32 devices in a mesh: gx: 8 (over y, x, core), ao: 4 (over z).
Axes of the slice: x: 2, y: 2, z: 4, core: 2. Of those that a mesh axis runs over, the one named last changes fastest.
Arguments:
- density: bfloat16 [384, 128, 1024], P('ao', 'gx'), may hold values from 0 to 2
- kernel: bfloat16 [384, 384], replicated, may hold values from -0.0102062073 to 0.0102062073
- neighbours: int32 [384, 6], replicated, may hold values from 0 to 383, as said below
- weights: int32 [384, 6], replicated, may hold values from 1 to 3
- signs: int32 [2, 384], replicated, may hold values from 0 to 1
- speeds: float32 [2, 384], replicated, may hold values from 0.05 to 0.2
Outputs:
- evolved: bfloat16 [384, 128, 1024], P('ao', 'gx')
The draws below stay inside these ranges and needn't reach their ends.
Inputs may be any that keep to these rules, and one draw needn't show every extreme that they name: `neighbours`: each entry names an orientation other than its own row's.
All inputs are finite; a program needn't handle non-finite values.
Results may differ from the reference program's by a relative error of at most 0.0052.
Values may be sent and summed in bfloat16 or wider, within the bound.
No kernel may reach another device: no remote copies, remote signals or barrier semaphores. Data moves between devices by JAX's collectives and lax.ppermute only.
A program may use at most 128 MiB of HBM per device.

```python
import math
import jax
import jax.numpy as jnp

ORIENT = 384
NEIGHBOURS = 6
COLUMNS = 1024
TIME_STEPS = 3
ROWS = 128


def draw_neighbours(key, part):
    offsets = jax.random.randint(key, (ORIENT, NEIGHBOURS), 1, ORIENT)
    labels = jnp.arange(ORIENT, dtype=jnp.int32)
    return ((labels[:, None] + offsets) % ORIENT).astype(jnp.int32)


def draw_kernel(key, part):
    spread = 0.199 / ORIENT ** 0.5
    values = jax.random.uniform(key, (ORIENT, ORIENT), jnp.float32, -1.0, 1.0)
    return (spread * values).astype(jnp.bfloat16)


def place_ends(entries, rng, low, largest):
    extent = entries.shape
    spot = [jax.random.randint(jax.random.fold_in(rng, axis), (), 0, extent[axis]) for axis in range(len(extent))]
    entries = entries.at[tuple(spot)].set(low)
    longest = extent.index(max(extent))
    spot[longest] = (spot[longest] + 1) % extent[longest]
    return entries.at[tuple(spot)].set(largest)


def levels(key, extent, cuts, low, top_value):
    gain = 1.0
    for dim, blocks in cuts:
        draws = jax.random.uniform(jax.random.fold_in(jax.random.fold_in(key, 6), dim), (blocks,), jnp.float32, low / len(cuts), top_value / len(cuts))
        gain = gain * jnp.repeat(jnp.exp(draws), extent[dim] // blocks).reshape((-1,) + (1,) * (len(extent) - 1 - dim))
    return gain


def setup_inputs(seed: int = 0) -> dict:
    key_list = jax.random.split(jax.random.key(seed), 7)
    return {
        "density": jnp.clip(2.0 * jax.random.uniform(key_list[0], (ORIENT, ROWS, COLUMNS), jnp.float32) ** levels(key_list[0], (ORIENT, ROWS, COLUMNS), ((0, 4), (1, 8)), -0.2, 0.2), 0.0, 2.0).astype(jnp.bfloat16),
        "kernel": draw_kernel(jax.random.fold_in(key_list[6], 71), 0),
        "neighbours": draw_neighbours(jax.random.fold_in(key_list[6], 71), 0),
        "weights": place_ends(jax.random.randint(key_list[3], (ORIENT, NEIGHBOURS), 1, 4), jax.random.fold_in(key_list[3], 1), 1, 3).astype(jnp.int32),
        "signs": place_ends(jax.random.randint(key_list[4], (2, ORIENT), 0, 2), jax.random.fold_in(key_list[4], 1), 0, 1).astype(jnp.int32),
        "speeds": jnp.clip(jnp.exp(jax.random.uniform(key_list[5], (2, ORIENT), jnp.float32, math.log(0.05), math.log(0.2))), 0.05, 0.2),
    }


rotation_rate = 0.05


def upwind(centre, behind_one, behind_two, ahead_one, ahead_two, direction, speed):
    rear = 0.5 * (3.0 * centre - 4.0 * behind_one + behind_two)
    front = 0.5 * (3.0 * centre - 4.0 * ahead_one + ahead_two)
    return speed * jnp.where(direction == 1, rear, front)


def stencil_matrix(neighbours, weights):
    number = neighbours.shape[0]
    labels = jnp.arange(number, dtype=jnp.int32)
    matches = (neighbours[:, :, None] == labels[None, None, :]).astype(jnp.float32)
    scaled = weights.astype(jnp.float32)
    coupled = jnp.sum(scaled[:, :, None] * matches, axis=1)
    totals = jnp.sum(scaled, axis=1)
    identity = (labels[:, None] == labels[None, :]).astype(jnp.float32)
    return (coupled - totals[:, None] * identity).astype(jnp.bfloat16)


def rotate_cells(values, kernel, turn_matrix):
    potential = jnp.dot(kernel, values, preferred_element_type=jnp.float32)
    wide_values = values.astype(jnp.float32)
    drifted = (wide_values * (1.0 + potential)).astype(jnp.bfloat16)
    turned = jnp.dot(turn_matrix, drifted, preferred_element_type=jnp.float32)
    return (wide_values + rotation_rate * turned).astype(jnp.bfloat16)


def reference(density, kernel, neighbours, weights, signs, speeds):
    turn_matrix = stencil_matrix(neighbours, weights)
    current = density
    for section_index in range(TIME_STEPS):
        centre = current.astype(jnp.float32)
        along_rows = upwind(centre, jnp.roll(centre, 1, 1), jnp.roll(centre, 2, 1),
                            jnp.roll(centre, -1, 1), jnp.roll(centre, -2, 1),
                            signs[0][:, None, None], speeds[0][:, None, None])
        along_columns = upwind(centre, jnp.roll(centre, 1, 2), jnp.roll(centre, 2, 2),
                               jnp.roll(centre, -1, 2), jnp.roll(centre, -2, 2),
                               signs[1][:, None, None], speeds[1][:, None, None])
        advected = (centre - along_rows - along_columns).astype(jnp.bfloat16)
        layout_shape = advected.shape
        flattened = advected.reshape(layout_shape[0], -1)
        current = rotate_cells(flattened, kernel, turn_matrix).reshape(layout_shape)
    return current
```

```python
import functools

import jax
import jax.numpy as jnp
from jax import lax
from jax.experimental import pallas as pl
from jax.experimental.pallas import tpu as pltpu
from jax.sharding import PartitionSpec as P

TIME_STEPS = 3


rotation_rate = 0.05


def extended(value, sides, width):
    for axis, dim in sides:
        devices, length = (lax.axis_size(axis), value.shape[dim])
        up = [(i, (i + 1) % devices) for i in range(devices)]
        down = [(j, i) for i, j in up]
        last = lax.slice_in_dim(value, length - width, length, axis=dim)
        leading = lax.slice_in_dim(value, 0, width, axis=dim)
        before = lax.ppermute(last, axis, up)
        after = lax.ppermute(leading, axis, down)
        value = jnp.concatenate([before, value, after], axis=dim)
    return value


def upwind(centre, behind_one, behind_two, ahead_one, ahead_two, direction, speed):
    rear = 0.5 * (3.0 * centre - 4.0 * behind_one + behind_two)
    front = 0.5 * (3.0 * centre - 4.0 * ahead_one + ahead_two)
    return speed * jnp.where(direction == 1, rear, front)


def stencil_matrix(neighbours, weights):
    number = neighbours.shape[0]
    labels = jnp.arange(number, dtype=jnp.int32)
    matches = (neighbours[:, :, None] == labels[None, None, :]).astype(jnp.float32)
    scaled = weights.astype(jnp.float32)
    coupled = jnp.sum(scaled[:, :, None] * matches, axis=1)
    totals = jnp.sum(scaled, axis=1)
    identity = (labels[:, None] == labels[None, :]).astype(jnp.float32)
    return (coupled - totals[:, None] * identity).astype(jnp.bfloat16)


def rotate_block(block, kernel, turn_matrix):
    block_shape = block.shape
    values = block.reshape(block_shape[0], -1)
    potential = jnp.dot(kernel, values, preferred_element_type=jnp.float32)
    wide_values = values.astype(jnp.float32)
    drifted = (wide_values * (1.0 + potential)).astype(jnp.bfloat16)
    turned = jnp.dot(turn_matrix, drifted, preferred_element_type=jnp.float32)
    return (wide_values + rotation_rate * turned).astype(jnp.bfloat16).reshape(block_shape)


def per_device(density, kernel, neighbours, weights, signs, speeds):
    turn_matrix = stencil_matrix(neighbours, weights)
    share = density.shape[0]
    offset = lax.axis_index("ao") * share
    local_signs = lax.dynamic_slice_in_dim(signs, offset, share, 1)
    local_speeds = lax.dynamic_slice_in_dim(speeds, offset, share, 1)
    current = density
    for section_index in range(TIME_STEPS):
        widened = extended(current, (("gx", 1),), 2).astype(jnp.float32)
        centre = current.astype(jnp.float32)
        along_rows = upwind(
            centre,
            widened[:, 1:-3],
            widened[:, :-4],
            widened[:, 3:-1],
            widened[:, 4:],
            local_signs[0][:, None, None],
            local_speeds[0][:, None, None],
        )
        along_columns = upwind(
            centre,
            jnp.roll(centre, 1, 2),
            jnp.roll(centre, 2, 2),
            jnp.roll(centre, -1, 2),
            jnp.roll(centre, -2, 2),
            local_signs[1][:, None, None],
            local_speeds[1][:, None, None],
        )
        advected = (centre - along_rows - along_columns).astype(jnp.bfloat16)
        current = lax.all_to_all(
            rotate_block(
                lax.all_to_all(advected, "ao", split_axis=2, concat_axis=0, tiled=True),
                kernel,
                turn_matrix,
            ),
            "ao",
            split_axis=0,
            concat_axis=2,
            tiled=True,
        )
    return current


LANES = 128
REACH = 2 * TIME_STEPS
GROUP = 8
SLOT = LANES // GROUP


def pack_kernel(place, main_ref, before_ref, after_ref, out_ref, main, sides):
    orients, rows, _ = main_ref.shape
    lane = lax.broadcasted_iota(jnp.int32, (orients, LANES), 1)
    main[...] = main_ref[...].astype(jnp.float32).reshape(orients * rows, LANES)
    wide_lane = lax.broadcasted_iota(jnp.int32, (orients * rows, LANES), 1)
    sides[...] = jnp.where(
        wide_lane < LANES // 2,
        after_ref[...].astype(jnp.float32).reshape(orients * rows, LANES),
        before_ref[...].astype(jnp.float32).reshape(orients * rows, LANES),
    )
    owner = ((lane + SLOT // 2) % LANES) // SLOT
    for group in range(rows // GROUP):
        packed = jnp.zeros((orients, LANES), jnp.float32)
        for slot in range(GROUP):
            row = group * GROUP + slot
            out_ref[1 + row] = main[pl.ds(row, orients, stride=rows), :].astype(jnp.bfloat16)
            edge = pltpu.roll(sides[pl.ds(row, orients, stride=rows), :], SLOT * slot, 1)
            packed = jnp.where(owner == slot, edge, packed)
        out_ref[0 if group == 0 else rows + 1] = packed.astype(jnp.bfloat16)


def pack(density, place, shift, part, devices, parts):
    share, rows, columns = density.shape
    tiles = columns // LANES
    step = 32

    def tile(offset):
        def index(block, place_ref):
            target = lax.rem(place_ref[0] + shift, devices)
            return block, 0, lax.rem(target * parts + part + offset + tiles, tiles)

        return pl.BlockSpec((step, rows, LANES), index)

    return pl.pallas_call(
        pack_kernel,
        grid_spec=pltpu.PrefetchScalarGridSpec(
            num_scalar_prefetch=1,
            grid=(share // step,),
            in_specs=[tile(0), tile(-1), tile(1)],
            out_specs=pl.BlockSpec((rows + 2, step, LANES), lambda block, place_ref: (0, block, 0)),
            scratch_shapes=[pltpu.VMEM((step * rows, LANES), jnp.float32)] * 2,
        ),
        out_shape=jax.ShapeDtypeStruct((rows + 2, share, LANES), jnp.bfloat16),
        name="pack",
    )(place, density, density, density)


def unpack_kernel(devices, place, *refs):
    blocks, out_ref, wide = refs[:devices], refs[-2], refs[-1]
    rows, share, _ = blocks[0].shape
    for shift in range(devices):

        @pl.when(pl.program_id(0) == shift)
        def _():
            wide[...] = blocks[shift][...].astype(jnp.float32).reshape(rows * share, LANES)
            for orient in range(share):
                out_ref[orient] = wide[pl.ds(orient, rows, stride=share), :].astype(jnp.bfloat16)


def unpack(blocks, place, part, parts, shape, before):
    devices = len(blocks)
    rows, share, _ = blocks[0].shape

    def index(shift, place_ref):
        return 0, 0, lax.rem(place_ref[0] + shift, devices) * parts + part

    whole = pl.BlockSpec(blocks[0].shape, lambda shift, place_ref: (0, 0, 0))
    earlier = () if before is None else (before,)
    return pl.pallas_call(
        functools.partial(unpack_kernel, devices),
        grid_spec=pltpu.PrefetchScalarGridSpec(
            num_scalar_prefetch=1,
            grid=(devices,),
            in_specs=[whole] * devices + [pl.BlockSpec(memory_space=pl.ANY)] * len(earlier),
            out_specs=pl.BlockSpec((share, rows, LANES), index),
            scratch_shapes=[pltpu.VMEM((rows * share, LANES), jnp.float32)],
        ),
        out_shape=jax.ShapeDtypeStruct(shape, jnp.bfloat16),
        input_output_aliases={1 + devices: 0} if earlier else {},
        name="unpack",
    )(place, *blocks, *earlier)


def steps_kernel(devices, *refs):
    blocks = refs[:devices]
    above, below, kernel, turn, keep, by_row, by_column, choose = refs[devices : devices + 8]
    outs = refs[devices + 8 : 2 * devices + 8]
    first, second, advected = refs[2 * devices + 8 :]
    share = blocks[0].shape[1]
    number = share * devices
    rows = outs[0].shape[0]

    def turned_back(value, slot):
        return pltpu.roll(value.astype(jnp.float32), (LANES - SLOT * slot) % LANES, 1).astype(jnp.bfloat16)

    for index in range(rows + 2 * REACH):
        row = index - REACH
        slot = row % GROUP
        if row < 0:
            first[index, :, :LANES] = above[index]
            first[index, :, LANES:] = turned_back(above[REACH], slot)
        elif row >= rows:
            first[index, :, :LANES] = below[1 + row - rows]
            first[index, :, LANES:] = turned_back(below[0], slot)
        else:
            for part in range(devices):
                span = slice(part * share, (part + 1) * share)
                first[index, span, :LANES] = blocks[part][1 + row]
                first[index, span, LANES:] = turned_back(blocks[part][0 if row < GROUP else rows + 1], slot)

    block = 48

    def advect(source, row, tiles, target, column):
        lane = lax.broadcasted_iota(jnp.int32, (block, LANES), 1)
        for start in range(0, number, block):
            span = slice(start, start + block)
            forward_row = choose[0, span] > 0
            forward_column = choose[1, span] > 0
            depth = jnp.where(forward_column, lane, LANES - 1 - lane)
            edge_one, edge_two = depth < 1, depth < 2
            centres, ones, twos = [], [], []
            for tile in range(2):
                centre = source[row + 2, span, tile * LANES : (tile + 1) * LANES].astype(jnp.float32)
                centres.append(centre)
                ones.append(jnp.where(forward_column, pltpu.roll(centre, 1, 1), pltpu.roll(centre, LANES - 1, 1)))
                twos.append(jnp.where(forward_column, pltpu.roll(centre, 2, 1), pltpu.roll(centre, LANES - 2, 1)))
            for tile in range(tiles):
                lanes = slice(tile * LANES, (tile + 1) * LANES)

                def at(offset):
                    return source[row + 2 + offset, span, lanes].astype(jnp.float32)

                row_one = jnp.where(forward_row, at(-1), at(1))
                row_two = jnp.where(forward_row, at(-2), at(2))
                column_one = jnp.where(edge_one, ones[1 - tile], ones[tile])
                column_two = jnp.where(edge_two, twos[1 - tile], twos[tile])
                value = (
                    keep[span] * centres[tile]
                    + by_row[span] * (row_one - 0.25 * row_two)
                    + by_column[span] * (column_one - 0.25 * column_two)
                )
                target[span, column + tile * LANES : column + (tile + 1) * LANES] = value.astype(jnp.bfloat16)

    def rotate(values):
        potential = jnp.dot(kernel[...], values[...], preferred_element_type=jnp.float32)
        drifted = (values[...].astype(jnp.float32) * (1.0 + potential)).astype(jnp.bfloat16)
        turned = jnp.dot(turn[...], drifted, preferred_element_type=jnp.float32)
        return (values[...].astype(jnp.float32) + rotation_rate * turned).astype(jnp.bfloat16)

    buffers = [first, second]
    for step in range(TIME_STEPS - 1):
        source, target = buffers[step % 2], buffers[(step + 1) % 2]

        @pl.loop(0, (rows + 2 * REACH - 4 * (step + 1)) // 2)
        def _(pair):
            row = 2 * pair
            for half in range(2):
                advect(source, row + half, 2, advected.at[half], 0)
            for half in range(2):
                target[row + half] = rotate(advected.at[half])

    source = buffers[(TIME_STEPS - 1) % 2]

    @pl.loop(0, rows // 4)
    def _(quad):
        row = 4 * quad
        for half in range(2):
            for side in range(2):
                advect(source, row + 2 * half + side, 1, advected.at[half], side * LANES)
        for half in range(2):
            result = rotate(advected.at[half])
            for side in range(2):
                for part in range(devices):
                    outs[part][row + 2 * half + side] = result[
                        part * share : (part + 1) * share, side * LANES : (side + 1) * LANES
                    ]


def three_steps(blocks, above, below, kernel, turn, coefficients):
    devices = len(blocks)
    rows, share, _ = blocks[0].shape
    rows -= 2
    number = share * devices
    cells = (rows + 2 * REACH) * 2 * LANES
    vmem = pl.BlockSpec(memory_space=pltpu.VMEM)
    operands = (*blocks, above, below, kernel, turn, *coefficients)
    return pl.pallas_call(
        functools.partial(steps_kernel, devices),
        in_specs=[vmem] * len(operands),
        out_specs=[vmem] * devices,
        out_shape=[jax.ShapeDtypeStruct((rows, share, LANES), jnp.bfloat16)] * devices,
        scratch_shapes=[
            pltpu.VMEM((rows + 2 * REACH, number, 2 * LANES), jnp.bfloat16),
            pltpu.VMEM((rows + 2 * REACH - 4, number, 2 * LANES), jnp.bfloat16),
            pltpu.VMEM((2, number, 2 * LANES), jnp.bfloat16),
        ],
        compiler_params=pltpu.CompilerParams(vmem_limit_bytes=48 * 2**20),
        cost_estimate=pl.CostEstimate(
            flops=12 * number * number * cells, bytes_accessed=8 * 2**20, transcendentals=0
        ),
        name="three_steps",
    )(*operands)


def blocked(density, kernel, neighbours, weights, signs, speeds):
    devices = lax.axis_size("ao")
    share, rows, columns = density.shape
    parts = columns // devices // LANES
    here = lax.axis_index("ao")
    place = here.astype(jnp.int32).reshape(1)

    packed = [[pack(density, place, shift, part, devices, parts) for shift in range(devices)] for part in range(parts)]

    def turned(value, dim):
        pieces = [
            lax.dynamic_slice_in_dim(value, lax.rem(here - shift + devices, devices) * share, share, dim)
            for shift in range(devices)
        ]
        return jnp.concatenate(pieces, dim)

    turn = turned(turned(stencil_matrix(neighbours, weights), 0), 1)
    kernel = turned(turned(kernel, 0), 1)
    signs, speeds = turned(signs, 1), turned(speeds, 1)

    def spread(value):
        return jnp.broadcast_to(value[..., None], value.shape + (LANES,))

    coefficients = (
        spread(1.0 - 1.5 * (speeds[0] + speeds[1])),
        spread(2.0 * speeds[0]),
        spread(2.0 * speeds[1]),
        spread((signs == 1).astype(jnp.float32)),
    )

    size = lax.axis_size("gx")
    up = [(i, (i + 1) % size) for i in range(size)]
    down = [(j, i) for i, j in up]
    evolved = None
    arrived = None
    results = []
    for part in range(parts):
        blocks = packed[part]
        if arrived is not None:
            blocks, _ = lax.optimization_barrier((blocks, arrived))
        arrived = [blocks[0]] + [
            lax.ppermute(blocks[shift], "ao", [(i, (i + shift) % devices) for i in range(devices)])
            for shift in range(1, devices)
        ]
        above = lax.ppermute(jnp.concatenate([block[-(REACH + 1) :] for block in arrived], 1), "gx", up)
        below = lax.ppermute(jnp.concatenate([block[: REACH + 1] for block in arrived], 1), "gx", down)
        results.append(three_steps(arrived, above, below, kernel, turn, coefficients))
    for part in range(parts):
        result = results[part]
        returned = [result[0]] + [
            lax.ppermute(result[shift], "ao", [(i, (i - shift) % devices) for i in range(devices)])
            for shift in range(1, devices)
        ]
        evolved = unpack(returned, place, part, parts, density.shape, evolved)
    return evolved


def solution(mesh):
    in_specs = (P("ao", "gx", None), P(), P(), P(), P(), P())
    out_specs = P("ao", "gx", None)

    def run(density, *rest):
        share, rows, columns = (
            density.shape[0] // mesh.shape["ao"],
            density.shape[1] // mesh.shape["gx"],
            density.shape[2] // mesh.shape["ao"],
        )
        fits = columns % LANES == 0 and share % 32 == 0 and rows == 2 * GROUP
        body = jax.shard_map(
            blocked if fits else per_device, mesh=mesh, in_specs=in_specs, out_specs=out_specs, check_vma=False
        )
        return body(density, *rest)

    return run
```

```python
import functools

import jax
import jax.numpy as jnp
from jax import lax
from jax.experimental import pallas as pl
from jax.experimental.pallas import tpu as pltpu
from jax.sharding import PartitionSpec as P

TIME_STEPS = 3


rotation_rate = 0.05


def extended(value, sides, width):
    for axis, dim in sides:
        devices, length = (lax.axis_size(axis), value.shape[dim])
        up = [(i, (i + 1) % devices) for i in range(devices)]
        down = [(j, i) for i, j in up]
        last = lax.slice_in_dim(value, length - width, length, axis=dim)
        leading = lax.slice_in_dim(value, 0, width, axis=dim)
        before = lax.ppermute(last, axis, up)
        after = lax.ppermute(leading, axis, down)
        value = jnp.concatenate([before, value, after], axis=dim)
    return value


def upwind(centre, behind_one, behind_two, ahead_one, ahead_two, direction, speed):
    rear = 0.5 * (3.0 * centre - 4.0 * behind_one + behind_two)
    front = 0.5 * (3.0 * centre - 4.0 * ahead_one + ahead_two)
    return speed * jnp.where(direction == 1, rear, front)


def stencil_matrix(neighbours, weights):
    number = neighbours.shape[0]
    labels = jnp.arange(number, dtype=jnp.int32)
    matches = (neighbours[:, :, None] == labels[None, None, :]).astype(jnp.float32)
    scaled = weights.astype(jnp.float32)
    coupled = jnp.sum(scaled[:, :, None] * matches, axis=1)
    totals = jnp.sum(scaled, axis=1)
    identity = (labels[:, None] == labels[None, :]).astype(jnp.float32)
    return (coupled - totals[:, None] * identity).astype(jnp.bfloat16)


def rotate_block(block, kernel, turn_matrix):
    block_shape = block.shape
    values = block.reshape(block_shape[0], -1)
    potential = jnp.dot(kernel, values, preferred_element_type=jnp.float32)
    wide_values = values.astype(jnp.float32)
    drifted = (wide_values * (1.0 + potential)).astype(jnp.bfloat16)
    turned = jnp.dot(turn_matrix, drifted, preferred_element_type=jnp.float32)
    return (wide_values + rotation_rate * turned).astype(jnp.bfloat16).reshape(block_shape)


def per_device(density, kernel, neighbours, weights, signs, speeds):
    turn_matrix = stencil_matrix(neighbours, weights)
    share = density.shape[0]
    offset = lax.axis_index("ao") * share
    local_signs = lax.dynamic_slice_in_dim(signs, offset, share, 1)
    local_speeds = lax.dynamic_slice_in_dim(speeds, offset, share, 1)
    current = density
    for section_index in range(TIME_STEPS):
        widened = extended(current, (("gx", 1),), 2).astype(jnp.float32)
        centre = current.astype(jnp.float32)
        along_rows = upwind(
            centre,
            widened[:, 1:-3],
            widened[:, :-4],
            widened[:, 3:-1],
            widened[:, 4:],
            local_signs[0][:, None, None],
            local_speeds[0][:, None, None],
        )
        along_columns = upwind(
            centre,
            jnp.roll(centre, 1, 2),
            jnp.roll(centre, 2, 2),
            jnp.roll(centre, -1, 2),
            jnp.roll(centre, -2, 2),
            local_signs[1][:, None, None],
            local_speeds[1][:, None, None],
        )
        advected = (centre - along_rows - along_columns).astype(jnp.bfloat16)
        current = lax.all_to_all(
            rotate_block(
                lax.all_to_all(advected, "ao", split_axis=2, concat_axis=0, tiled=True),
                kernel,
                turn_matrix,
            ),
            "ao",
            split_axis=0,
            concat_axis=2,
            tiled=True,
        )
    return current


LANES = 128
REACH = 2 * TIME_STEPS
GROUP = 8
SLOT = LANES // GROUP


def pack_kernel(place, main_ref, before_ref, after_ref, out_ref, main, sides):
    orients, rows, _ = main_ref.shape
    lane = lax.broadcasted_iota(jnp.int32, (orients, LANES), 1)
    main[...] = main_ref[...].astype(jnp.float32).reshape(orients * rows, LANES)
    wide_lane = lax.broadcasted_iota(jnp.int32, (orients * rows, LANES), 1)
    sides[...] = jnp.where(
        wide_lane < LANES // 2,
        after_ref[...].astype(jnp.float32).reshape(orients * rows, LANES),
        before_ref[...].astype(jnp.float32).reshape(orients * rows, LANES),
    )
    owner = ((lane + SLOT // 2) % LANES) // SLOT
    for group in range(rows // GROUP):
        packed = jnp.zeros((orients, LANES), jnp.float32)
        for slot in range(GROUP):
            row = group * GROUP + slot
            out_ref[1 + row] = main[pl.ds(row, orients, stride=rows), :].astype(jnp.bfloat16)
            edge = pltpu.roll(sides[pl.ds(row, orients, stride=rows), :], SLOT * slot, 1)
            packed = jnp.where(owner == slot, edge, packed)
        out_ref[0 if group == 0 else rows + 1] = packed.astype(jnp.bfloat16)


def pack(density, place, shift, part, devices, parts):
    share, rows, columns = density.shape
    tiles = columns // LANES
    step = share

    def tile(offset):
        def index(block, place_ref):
            target = lax.rem(place_ref[0] + shift, devices)
            return block, 0, lax.rem(target * parts + part + offset + tiles, tiles)

        return pl.BlockSpec((step, rows, LANES), index)

    return pl.pallas_call(
        pack_kernel,
        grid_spec=pltpu.PrefetchScalarGridSpec(
            num_scalar_prefetch=1,
            grid=(share // step,),
            in_specs=[tile(0), tile(-1), tile(1)],
            out_specs=pl.BlockSpec((rows + 2, step, LANES), lambda block, place_ref: (0, block, 0)),
            scratch_shapes=[pltpu.VMEM((step * rows, LANES), jnp.float32)] * 2,
        ),
        out_shape=jax.ShapeDtypeStruct((rows + 2, share, LANES), jnp.bfloat16),
        name="pack",
    )(place, density, density, density)


def unpack_kernel(devices, place, *refs):
    blocks, out_ref, wide = refs[:devices], refs[-2], refs[-1]
    rows, share, _ = blocks[0].shape
    for shift in range(devices):

        @pl.when(pl.program_id(0) == shift)
        def _():
            wide[...] = blocks[shift][...].astype(jnp.float32).reshape(rows * share, LANES)
            for orient in range(share):
                out_ref[orient] = wide[pl.ds(orient, rows, stride=share), :].astype(jnp.bfloat16)


def unpack(blocks, place, part, parts, shape, before):
    devices = len(blocks)
    rows, share, _ = blocks[0].shape

    def index(shift, place_ref):
        return 0, 0, lax.rem(place_ref[0] + shift, devices) * parts + part

    whole = pl.BlockSpec(blocks[0].shape, lambda shift, place_ref: (0, 0, 0))
    earlier = () if before is None else (before,)
    return pl.pallas_call(
        functools.partial(unpack_kernel, devices),
        grid_spec=pltpu.PrefetchScalarGridSpec(
            num_scalar_prefetch=1,
            grid=(devices,),
            in_specs=[whole] * devices + [pl.BlockSpec(memory_space=pl.ANY)] * len(earlier),
            out_specs=pl.BlockSpec((share, rows, LANES), index),
            scratch_shapes=[pltpu.VMEM((rows * share, LANES), jnp.float32)],
        ),
        out_shape=jax.ShapeDtypeStruct(shape, jnp.bfloat16),
        input_output_aliases={1 + devices: 0} if earlier else {},
        name="unpack",
    )(place, *blocks, *earlier)


def steps_kernel(devices, *refs):
    blocks = refs[:devices]
    above, below, kernel, turn, coefficients = refs[devices : devices + 5]
    outs = refs[devices + 5 : 2 * devices + 5]
    buffers = refs[2 * devices + 5 : 2 * devices + 7]
    waiting = refs[2 * devices + 7 :]
    share = blocks[0].shape[1]
    number = share * devices
    rows = outs[0].shape[0]
    tiles = number // LANES

    def transposed(value_of):
        return jnp.concatenate([value_of(part).astype(jnp.float32) for part in range(devices)], 0).T

    def piece(ref, index, part):
        return ref[index, part * share : (part + 1) * share]

    def fill(first, last, value_of):
        for row in range(first, last):
            cells = transposed(lambda part: value_of(row, part))
            for tile in range(tiles):
                buffers[0][row + REACH, tile, 2 * GROUP : 2 * GROUP + LANES] = cells[
                    :, tile * LANES : (tile + 1) * LANES
                ]

    def fill_sides(first, last, value_of):
        cells = transposed(value_of)
        for row in range(first, last):
            slot = row % GROUP
            left, right = (SLOT * slot - GROUP) % LANES, SLOT * slot
            for tile in range(tiles):
                lanes = slice(tile * LANES, (tile + 1) * LANES)
                buffers[0][row + REACH, tile, GROUP : 2 * GROUP] = cells[left : left + GROUP, lanes]
                buffers[0][row + REACH, tile, 2 * GROUP + LANES : 3 * GROUP + LANES] = cells[
                    right : right + GROUP, lanes
                ]

    fill(-REACH, 0, lambda row, part: piece(above, row + REACH, part))
    fill(0, rows, lambda row, part: blocks[part][1 + row])
    fill(rows, rows + REACH, lambda row, part: piece(below, 1 + row - rows, part))
    fill_sides(-REACH, 0, lambda part: piece(above, REACH, part))
    fill_sides(0, GROUP, lambda part: blocks[part][0])
    fill_sides(GROUP, rows, lambda part: blocks[part][rows + 1])
    fill_sides(rows, rows + REACH, lambda part: piece(below, 0, part))

    def advect(source, index, start, length, target):
        for tile in range(tiles):
            lanes = slice(tile * LANES, (tile + 1) * LANES)
            keep, by_row, by_column, row_sign, column_sign = (coefficients[k : k + 1, lanes] for k in range(5))
            forward_row = jnp.broadcast_to(row_sign, (length, LANES)) > 0
            forward_column = jnp.broadcast_to(column_sign, (length, LANES)) > 0
            for half in range(2):

                def at(row, column):
                    return source[index + half + row, tile, start + column : start + column + length]

                row_one = jnp.where(forward_row, at(-1, 0), at(1, 0))
                row_two = jnp.where(forward_row, at(-2, 0), at(2, 0))
                column_one = jnp.where(forward_column, at(0, -1), at(0, 1))
                column_two = jnp.where(forward_column, at(0, -2), at(0, 2))
                value = (
                    keep * at(0, 0)
                    + by_row * (row_one - 0.25 * row_two)
                    + by_column * (column_one - 0.25 * column_two)
                )
                target[half * length : (half + 1) * length, lanes] = value.astype(jnp.bfloat16)

    def rotate(values):
        potential = jnp.dot(values, kernel[...], preferred_element_type=jnp.float32)
        drifted = (values.astype(jnp.float32) * (1.0 + potential)).astype(jnp.bfloat16)
        turned = jnp.dot(drifted, turn[...], preferred_element_type=jnp.float32)
        return (values.astype(jnp.float32) + rotation_rate * turned).astype(jnp.bfloat16)

    for step in range(TIME_STEPS):
        source, target = buffers[step % 2], buffers[(step + 1) % 2]
        last = step == TIME_STEPS - 1
        start, length = (2 * GROUP, LANES) if last else (GROUP, LANES + 2 * GROUP)
        low, pairs = 2 * (step + 1), rows // 2 + REACH - 2 * (step + 1)

        def finish(slot, index):
            result = rotate(waiting[slot][: 2 * length]).astype(jnp.float32)
            for half in range(2):
                cells = result[half * length : (half + 1) * length]
                if last:
                    back = cells.T.astype(jnp.bfloat16)
                    for part in range(devices):
                        outs[part][index - REACH + half] = back[part * share : (part + 1) * share]
                else:
                    for tile in range(tiles):
                        target[index + half, tile, start : start + length] = cells[
                            :, tile * LANES : (tile + 1) * LANES
                        ]

        advect(source, low, start, length, waiting[0])

        @pl.loop(0, pairs // 2)
        def _(turn_index):
            index = low + 4 * turn_index
            advect(source, index + 2, start, length, waiting[1])
            finish(0, index)
            advect(source, jnp.minimum(index + 4, low + 2 * pairs - 2), start, length, waiting[0])
            finish(1, index + 2)


def three_steps(blocks, above, below, kernel, turn, coefficients):
    devices = len(blocks)
    rows, share, _ = blocks[0].shape
    rows -= 2
    number = share * devices
    cells = (rows + 2 * REACH) * LANES
    vmem = pl.BlockSpec(memory_space=pltpu.VMEM)
    operands = (*blocks, above, below, kernel, turn, coefficients)
    return pl.pallas_call(
        functools.partial(steps_kernel, devices),
        in_specs=[vmem] * len(operands),
        out_specs=[vmem] * devices,
        out_shape=[jax.ShapeDtypeStruct((rows, share, LANES), jnp.bfloat16)] * devices,
        scratch_shapes=[
            *[pltpu.VMEM((rows + 2 * REACH, number // LANES, LANES + 4 * GROUP, LANES), jnp.float32)] * 2,
            *[pltpu.VMEM((2 * (LANES + 2 * GROUP), number), jnp.bfloat16)] * 2,
        ],
        compiler_params=pltpu.CompilerParams(vmem_limit_bytes=48 * 2**20),
        cost_estimate=pl.CostEstimate(
            flops=12 * number * number * cells, bytes_accessed=8 * 2**20, transcendentals=0
        ),
        name="three_steps",
    )(*operands)


def blocked(density, kernel, neighbours, weights, signs, speeds):
    devices = lax.axis_size("ao")
    share, rows, columns = density.shape
    parts = columns // devices // LANES
    here = lax.axis_index("ao")
    place = here.astype(jnp.int32).reshape(1)

    packed = [[pack(density, place, shift, part, devices, parts) for shift in range(devices)] for part in range(parts)]

    def turned(value, dim):
        pieces = [
            lax.dynamic_slice_in_dim(value, lax.rem(here - shift + devices, devices) * share, share, dim)
            for shift in range(devices)
        ]
        return jnp.concatenate(pieces, dim)

    turn = turned(turned(stencil_matrix(neighbours, weights), 0), 1)
    kernel = turned(turned(kernel, 0), 1)
    signs, speeds = turned(signs, 1), turned(speeds, 1)

    coefficients = jnp.stack(
        [
            1.0 - 1.5 * (speeds[0] + speeds[1]),
            2.0 * speeds[0],
            2.0 * speeds[1],
            (signs[0] == 1).astype(jnp.float32),
            (signs[1] == 1).astype(jnp.float32),
        ]
    )
    kernel, turn = kernel.T, turn.T

    size = lax.axis_size("gx")
    up = [(i, (i + 1) % size) for i in range(size)]
    down = [(j, i) for i, j in up]
    evolved = None
    arrived = None
    results = []
    for part in range(parts):
        blocks = packed[part]
        if arrived is not None:
            blocks, _ = lax.optimization_barrier((blocks, arrived))
        arrived = [blocks[0]] + [
            lax.ppermute(blocks[shift], "ao", [(i, (i + shift) % devices) for i in range(devices)])
            for shift in range(1, devices)
        ]
        if results:
            arrived, _ = lax.optimization_barrier((arrived, results[-1]))
        above = lax.ppermute(jnp.concatenate([block[-(REACH + 1) :] for block in arrived], 1), "gx", up)
        below = lax.ppermute(jnp.concatenate([block[: REACH + 1] for block in arrived], 1), "gx", down)
        results.append(three_steps(arrived, above, below, kernel, turn, coefficients))
    for part in range(parts):
        result = results[part]
        returned = [result[0]] + [
            lax.ppermute(result[shift], "ao", [(i, (i - shift) % devices) for i in range(devices)])
            for shift in range(1, devices)
        ]
        evolved = unpack(returned, place, part, parts, density.shape, evolved)
    return evolved


def solution(mesh):
    in_specs = (P("ao", "gx", None), P(), P(), P(), P(), P())
    out_specs = P("ao", "gx", None)

    def run(density, *rest):
        share, rows, columns = (
            density.shape[0] // mesh.shape["ao"],
            density.shape[1] // mesh.shape["gx"],
            density.shape[2] // mesh.shape["ao"],
        )
        fits = columns % LANES == 0 and share % 32 == 0 and rows == 2 * GROUP
        body = jax.shard_map(
            blocked if fits else per_device, mesh=mesh, in_specs=in_specs, out_specs=out_specs, check_vma=False
        )
        return body(density, *rest)

    return run
```

```python
import functools

import jax
import jax.numpy as jnp
from jax import lax
from jax.experimental import pallas as pl
from jax.experimental.pallas import tpu as pltpu
from jax.sharding import PartitionSpec as P

TIME_STEPS = 3


rotation_rate = 0.05


def extended(value, sides, width):
    for axis, dim in sides:
        devices, length = (lax.axis_size(axis), value.shape[dim])
        up = [(i, (i + 1) % devices) for i in range(devices)]
        down = [(j, i) for i, j in up]
        last = lax.slice_in_dim(value, length - width, length, axis=dim)
        leading = lax.slice_in_dim(value, 0, width, axis=dim)
        before = lax.ppermute(last, axis, up)
        after = lax.ppermute(leading, axis, down)
        value = jnp.concatenate([before, value, after], axis=dim)
    return value


def upwind(centre, behind_one, behind_two, ahead_one, ahead_two, direction, speed):
    rear = 0.5 * (3.0 * centre - 4.0 * behind_one + behind_two)
    front = 0.5 * (3.0 * centre - 4.0 * ahead_one + ahead_two)
    return speed * jnp.where(direction == 1, rear, front)


def stencil_matrix(neighbours, weights):
    number = neighbours.shape[0]
    labels = jnp.arange(number, dtype=jnp.int32)
    matches = (neighbours[:, :, None] == labels[None, None, :]).astype(jnp.float32)
    scaled = weights.astype(jnp.float32)
    coupled = jnp.sum(scaled[:, :, None] * matches, axis=1)
    totals = jnp.sum(scaled, axis=1)
    identity = (labels[:, None] == labels[None, :]).astype(jnp.float32)
    return (coupled - totals[:, None] * identity).astype(jnp.bfloat16)


def rotate_block(block, kernel, turn_matrix):
    block_shape = block.shape
    values = block.reshape(block_shape[0], -1)
    potential = jnp.dot(kernel, values, preferred_element_type=jnp.float32)
    wide_values = values.astype(jnp.float32)
    drifted = (wide_values * (1.0 + potential)).astype(jnp.bfloat16)
    turned = jnp.dot(turn_matrix, drifted, preferred_element_type=jnp.float32)
    return (wide_values + rotation_rate * turned).astype(jnp.bfloat16).reshape(block_shape)


def per_device(density, kernel, neighbours, weights, signs, speeds):
    turn_matrix = stencil_matrix(neighbours, weights)
    share = density.shape[0]
    offset = lax.axis_index("ao") * share
    local_signs = lax.dynamic_slice_in_dim(signs, offset, share, 1)
    local_speeds = lax.dynamic_slice_in_dim(speeds, offset, share, 1)
    current = density
    for section_index in range(TIME_STEPS):
        widened = extended(current, (("gx", 1),), 2).astype(jnp.float32)
        centre = current.astype(jnp.float32)
        along_rows = upwind(
            centre,
            widened[:, 1:-3],
            widened[:, :-4],
            widened[:, 3:-1],
            widened[:, 4:],
            local_signs[0][:, None, None],
            local_speeds[0][:, None, None],
        )
        along_columns = upwind(
            centre,
            jnp.roll(centre, 1, 2),
            jnp.roll(centre, 2, 2),
            jnp.roll(centre, -1, 2),
            jnp.roll(centre, -2, 2),
            local_signs[1][:, None, None],
            local_speeds[1][:, None, None],
        )
        advected = (centre - along_rows - along_columns).astype(jnp.bfloat16)
        current = lax.all_to_all(
            rotate_block(
                lax.all_to_all(advected, "ao", split_axis=2, concat_axis=0, tiled=True),
                kernel,
                turn_matrix,
            ),
            "ao",
            split_axis=0,
            concat_axis=2,
            tiled=True,
        )
    return current


LANES = 128
REACH = 2 * TIME_STEPS
GROUP = 8
SLOT = LANES // GROUP
TURNS = 4


def pack_kernel(place, main_ref, before_ref, after_ref, out_ref, main, sides):
    orients, rows, _ = main_ref.shape
    lane = lax.broadcasted_iota(jnp.int32, (orients, LANES), 1)
    main[...] = main_ref[...].astype(jnp.float32).reshape(orients * rows, LANES)
    wide_lane = lax.broadcasted_iota(jnp.int32, (orients * rows, LANES), 1)
    sides[...] = jnp.where(
        wide_lane < LANES // 2,
        after_ref[...].astype(jnp.float32).reshape(orients * rows, LANES),
        before_ref[...].astype(jnp.float32).reshape(orients * rows, LANES),
    )
    owner = ((lane + SLOT // 2) % LANES) // SLOT
    for group in range(rows // GROUP):
        packed = jnp.zeros((orients, LANES), jnp.float32)
        for slot in range(GROUP):
            row = group * GROUP + slot
            out_ref[1 + row] = main[pl.ds(row, orients, stride=rows), :].astype(jnp.bfloat16)
            edge = pltpu.roll(sides[pl.ds(row, orients, stride=rows), :], SLOT * slot, 1)
            packed = jnp.where(owner == slot, edge, packed)
        out_ref[0 if group == 0 else rows + 1] = packed.astype(jnp.bfloat16)


def pack(density, place, shift, part, devices, parts):
    share, rows, columns = density.shape
    tiles = columns // LANES
    step = share

    def tile(offset):
        def index(block, place_ref):
            target = lax.rem(place_ref[0] + shift, devices)
            return block, 0, lax.rem(target * parts + part + offset + tiles, tiles)

        return pl.BlockSpec((step, rows, LANES), index)

    return pl.pallas_call(
        pack_kernel,
        grid_spec=pltpu.PrefetchScalarGridSpec(
            num_scalar_prefetch=1,
            grid=(share // step,),
            in_specs=[tile(0), tile(-1), tile(1)],
            out_specs=pl.BlockSpec((rows + 2, step, LANES), lambda block, place_ref: (0, block, 0)),
            scratch_shapes=[pltpu.VMEM((step * rows, LANES), jnp.float32)] * 2,
        ),
        out_shape=jax.ShapeDtypeStruct((rows + 2, share, LANES), jnp.bfloat16),
        name="pack",
    )(place, density, density, density)


def unpack_kernel(devices, part, parts, place, *refs):
    blocks, out_ref, wide, staged, sems = refs[:devices], *refs[-4:]
    rows, share, _ = blocks[0].shape
    copies = []
    for shift in range(devices):
        wide[...] = blocks[shift][...].astype(jnp.float32).reshape(rows * share, LANES)
        for orient in range(share):
            staged[shift, orient] = wide[pl.ds(orient, rows, stride=share), :].astype(jnp.bfloat16)
        tile = lax.rem(place[0] + shift, devices) * parts + part
        copies.append(
            pltpu.make_async_copy(
                staged.at[shift],
                out_ref.at[:, :, pl.ds(pl.multiple_of(tile * LANES, LANES), LANES)],
                sems.at[shift],
            )
        )
        copies[-1].start()
    for copy in copies:
        copy.wait()


def unpack(blocks, place, part, parts, shape, before):
    devices = len(blocks)
    rows, share, _ = blocks[0].shape
    earlier = () if before is None else (before,)
    return pl.pallas_call(
        functools.partial(unpack_kernel, devices, part, parts),
        in_specs=[pl.BlockSpec(memory_space=pltpu.SMEM)]
        + [pl.BlockSpec(memory_space=pltpu.VMEM)] * devices
        + [pl.BlockSpec(memory_space=pl.ANY)] * len(earlier),
        out_specs=pl.BlockSpec(memory_space=pl.ANY),
        scratch_shapes=[
            pltpu.VMEM((rows * share, LANES), jnp.float32),
            pltpu.VMEM((devices, share, rows, LANES), jnp.bfloat16),
            pltpu.SemaphoreType.DMA((devices,)),
        ],
        out_shape=jax.ShapeDtypeStruct(shape, jnp.bfloat16),
        input_output_aliases={1 + devices: 0} if earlier else {},
        compiler_params=pltpu.CompilerParams(vmem_limit_bytes=16 * 2**20),
        name="unpack",
    )(place, *blocks, *earlier)


def steps_kernel(devices, *refs):
    blocks = refs[:devices]
    above, below, kernel, turn, coefficients = refs[devices : devices + 5]
    outs = refs[devices + 5 : 2 * devices + 5]
    buffers = refs[2 * devices + 5 : 2 * devices + 7]
    waiting = refs[2 * devices + 7 :]
    share = blocks[0].shape[1]
    number = share * devices
    rows = outs[0].shape[0]
    tiles = number // LANES

    def transposed(value_of):
        return jnp.concatenate([value_of(part).astype(jnp.float32) for part in range(devices)], 0).T

    def piece(ref, index, part):
        return ref[index, part * share : (part + 1) * share]

    def fill(first, last, value_of):
        for row in range(first, last):
            cells = transposed(lambda part: value_of(row, part))
            for tile in range(tiles):
                buffers[0][row + REACH, tile, 2 * GROUP : 2 * GROUP + LANES] = cells[
                    :, tile * LANES : (tile + 1) * LANES
                ]

    def fill_sides(first, last, value_of):
        cells = transposed(value_of)
        for row in range(first, last):
            slot = row % GROUP
            left, right = (SLOT * slot - GROUP) % LANES, SLOT * slot
            for tile in range(tiles):
                lanes = slice(tile * LANES, (tile + 1) * LANES)
                buffers[0][row + REACH, tile, GROUP : 2 * GROUP] = cells[left : left + GROUP, lanes]
                buffers[0][row + REACH, tile, 2 * GROUP + LANES : 3 * GROUP + LANES] = cells[
                    right : right + GROUP, lanes
                ]

    fill(-REACH, 0, lambda row, part: piece(above, row + REACH, part))
    fill(0, rows, lambda row, part: blocks[part][1 + row])
    fill(rows, rows + REACH, lambda row, part: piece(below, 1 + row - rows, part))
    fill_sides(-REACH, 0, lambda part: piece(above, REACH, part))
    fill_sides(0, GROUP, lambda part: blocks[part][0])
    fill_sides(GROUP, rows, lambda part: blocks[part][rows + 1])
    fill_sides(rows, rows + REACH, lambda part: piece(below, 0, part))

    def advect(source, index, start, length, together, target):
        for tile in range(tiles):
            lanes = slice(tile * LANES, (tile + 1) * LANES)
            keep, by_row, by_column, row_sign, column_sign = (coefficients[k : k + 1, lanes] for k in range(5))
            forward_row = jnp.broadcast_to(row_sign, (length, LANES)) > 0
            forward_column = jnp.broadcast_to(column_sign, (length, LANES)) > 0
            for half in range(together):

                def at(row, column):
                    return source[index + half + row, tile, start + column : start + column + length]

                row_one = jnp.where(forward_row, at(-1, 0), at(1, 0))
                row_two = jnp.where(forward_row, at(-2, 0), at(2, 0))
                column_one = jnp.where(forward_column, at(0, -1), at(0, 1))
                column_two = jnp.where(forward_column, at(0, -2), at(0, 2))
                value = (
                    keep * at(0, 0)
                    + by_row * (row_one - 0.25 * row_two)
                    + by_column * (column_one - 0.25 * column_two)
                )
                target[half * length : (half + 1) * length, lanes] = value.astype(jnp.bfloat16)

    def rotate(values):
        potential = jnp.dot(values, kernel[...], preferred_element_type=jnp.float32)
        drifted = (values.astype(jnp.float32) * (1.0 + potential)).astype(jnp.bfloat16)
        turned = jnp.dot(drifted, turn[...], preferred_element_type=jnp.float32)
        return (values.astype(jnp.float32) + rotation_rate * turned).astype(jnp.bfloat16)

    for step in range(TIME_STEPS):
        source, target = buffers[step % 2], buffers[(step + 1) % 2]
        last = step == TIME_STEPS - 1
        start, length = (2 * GROUP, LANES) if last else (GROUP, LANES + 2 * GROUP)
        low = 2 * (step + 1)
        turns = TURNS
        together = (rows + 2 * REACH - 2 * low) // turns

        def finish(slot, index):
            result = rotate(waiting[slot][: together * length]).astype(jnp.float32)
            for half in range(together):
                cells = result[half * length : (half + 1) * length]
                if last:
                    back = cells.T.astype(jnp.bfloat16)
                    for part in range(devices):
                        outs[part][index - REACH + half] = back[part * share : (part + 1) * share]
                else:
                    for tile in range(tiles):
                        target[index + half, tile, start : start + length] = cells[
                            :, tile * LANES : (tile + 1) * LANES
                        ]

        advect(source, low, start, length, together, waiting[0])

        @pl.loop(0, (turns - 1) // 2)
        def _(turn_index):
            index = low + 2 * together * turn_index
            advect(source, index + together, start, length, together, waiting[1])
            finish(0, index)
            advect(source, index + 2 * together, start, length, together, waiting[0])
            finish(1, index + together)

        index = low + together * 2 * ((turns - 1) // 2)
        if turns % 2 == 0:
            advect(source, index + together, start, length, together, waiting[1])
        finish(0, index)
        if turns % 2 == 0:
            finish(1, index + together)


def three_steps(blocks, above, below, kernel, turn, coefficients):
    devices = len(blocks)
    rows, share, _ = blocks[0].shape
    rows -= 2
    number = share * devices
    cells = (rows + 2 * REACH) * LANES
    vmem = pl.BlockSpec(memory_space=pltpu.VMEM)
    operands = (*blocks, above, below, kernel, turn, coefficients)
    return pl.pallas_call(
        functools.partial(steps_kernel, devices),
        in_specs=[vmem] * len(operands),
        out_specs=[vmem] * devices,
        out_shape=[jax.ShapeDtypeStruct((rows, share, LANES), jnp.bfloat16)] * devices,
        scratch_shapes=[
            *[pltpu.VMEM((rows + 2 * REACH, number // LANES, LANES + 4 * GROUP, LANES), jnp.float32)] * 2,
            *[pltpu.VMEM(((rows + 2 * REACH - 4) // TURNS * (LANES + 2 * GROUP), number), jnp.bfloat16)] * 2,
        ],
        compiler_params=pltpu.CompilerParams(vmem_limit_bytes=48 * 2**20),
        cost_estimate=pl.CostEstimate(
            flops=12 * number * number * cells, bytes_accessed=8 * 2**20, transcendentals=0
        ),
        name="three_steps",
    )(*operands)


def blocked(density, kernel, neighbours, weights, signs, speeds):
    devices = lax.axis_size("ao")
    share, rows, columns = density.shape
    parts = columns // devices // LANES
    here = lax.axis_index("ao")
    place = here.astype(jnp.int32).reshape(1)

    packed = [[pack(density, place, shift, part, devices, parts) for shift in range(devices)] for part in range(parts)]

    def turned(value, dim):
        pieces = [
            lax.dynamic_slice_in_dim(value, lax.rem(here - shift + devices, devices) * share, share, dim)
            for shift in range(devices)
        ]
        return jnp.concatenate(pieces, dim)

    turn = turned(turned(stencil_matrix(neighbours, weights), 0), 1)
    kernel = turned(turned(kernel, 0), 1)
    signs, speeds = turned(signs, 1), turned(speeds, 1)

    coefficients = jnp.stack(
        [
            1.0 - 1.5 * (speeds[0] + speeds[1]),
            2.0 * speeds[0],
            2.0 * speeds[1],
            (signs[0] == 1).astype(jnp.float32),
            (signs[1] == 1).astype(jnp.float32),
        ]
    )
    kernel, turn = kernel.T, turn.T

    size = lax.axis_size("gx")
    up = [(i, (i + 1) % size) for i in range(size)]
    down = [(j, i) for i, j in up]
    def ahead(value, shift):
        return lax.ppermute(value, "ao", [(i, (i + shift) % devices) for i in range(devices)])

    def after(value, *earlier):
        return lax.optimization_barrier((value, *earlier))[0]

    received = []
    for part in range(parts):
        blocks = packed[part]
        if received:
            earlier = received[-1]
            blocks = [after(block, early) for block, early in zip(blocks, earlier)]
        received.append([blocks[0]] + [ahead(blocks[shift], shift) for shift in range(1, devices)])
    results = []
    for part in range(parts):
        arrived = received[part]
        edges = [after(block, results[-1]) for block in arrived] if results else arrived
        above = lax.ppermute(jnp.concatenate([block[-(REACH + 1) :] for block in edges], 1), "gx", up)
        below = lax.ppermute(jnp.concatenate([block[: REACH + 1] for block in edges], 1), "gx", down)
        results.append(three_steps(arrived, above, below, kernel, turn, coefficients))
    evolved = None
    for part in range(parts):
        result = results[part]
        returned = [result[0]] + [ahead(result[shift], devices - shift) for shift in range(1, devices)]
        evolved = unpack(returned, place, part, parts, density.shape, evolved)
    return evolved


def solution(mesh):
    in_specs = (P("ao", "gx", None), P(), P(), P(), P(), P())
    out_specs = P("ao", "gx", None)

    def run(density, *rest):
        share, rows, columns = (
            density.shape[0] // mesh.shape["ao"],
            density.shape[1] // mesh.shape["gx"],
            density.shape[2] // mesh.shape["ao"],
        )
        fits = columns % LANES == 0 and share % 32 == 0 and rows == 2 * GROUP
        body = jax.shard_map(
            blocked if fits else per_device, mesh=mesh, in_specs=in_specs, out_specs=out_specs, check_vma=False
        )
        return body(density, *rest)

    return run
```

```python
import functools

import jax
import jax.numpy as jnp
from jax import lax
from jax.experimental import pallas as pl
from jax.experimental.pallas import tpu as pltpu
from jax.sharding import PartitionSpec as P

TIME_STEPS = 3


rotation_rate = 0.05


def extended(value, sides, width):
    for axis, dim in sides:
        devices, length = (lax.axis_size(axis), value.shape[dim])
        up = [(i, (i + 1) % devices) for i in range(devices)]
        down = [(j, i) for i, j in up]
        last = lax.slice_in_dim(value, length - width, length, axis=dim)
        leading = lax.slice_in_dim(value, 0, width, axis=dim)
        before = lax.ppermute(last, axis, up)
        after = lax.ppermute(leading, axis, down)
        value = jnp.concatenate([before, value, after], axis=dim)
    return value


def upwind(centre, behind_one, behind_two, ahead_one, ahead_two, direction, speed):
    rear = 0.5 * (3.0 * centre - 4.0 * behind_one + behind_two)
    front = 0.5 * (3.0 * centre - 4.0 * ahead_one + ahead_two)
    return speed * jnp.where(direction == 1, rear, front)


def stencil_matrix(neighbours, weights):
    number = neighbours.shape[0]
    labels = jnp.arange(number, dtype=jnp.int32)
    matches = (neighbours[:, :, None] == labels[None, None, :]).astype(jnp.float32)
    scaled = weights.astype(jnp.float32)
    coupled = jnp.sum(scaled[:, :, None] * matches, axis=1)
    totals = jnp.sum(scaled, axis=1)
    identity = (labels[:, None] == labels[None, :]).astype(jnp.float32)
    return (coupled - totals[:, None] * identity).astype(jnp.bfloat16)


def rotate_block(block, kernel, turn_matrix):
    block_shape = block.shape
    values = block.reshape(block_shape[0], -1)
    potential = jnp.dot(kernel, values, preferred_element_type=jnp.float32)
    wide_values = values.astype(jnp.float32)
    drifted = (wide_values * (1.0 + potential)).astype(jnp.bfloat16)
    turned = jnp.dot(turn_matrix, drifted, preferred_element_type=jnp.float32)
    return (wide_values + rotation_rate * turned).astype(jnp.bfloat16).reshape(block_shape)


def per_device(density, kernel, neighbours, weights, signs, speeds):
    turn_matrix = stencil_matrix(neighbours, weights)
    share = density.shape[0]
    offset = lax.axis_index("ao") * share
    local_signs = lax.dynamic_slice_in_dim(signs, offset, share, 1)
    local_speeds = lax.dynamic_slice_in_dim(speeds, offset, share, 1)
    current = density
    for section_index in range(TIME_STEPS):
        widened = extended(current, (("gx", 1),), 2).astype(jnp.float32)
        centre = current.astype(jnp.float32)
        along_rows = upwind(
            centre,
            widened[:, 1:-3],
            widened[:, :-4],
            widened[:, 3:-1],
            widened[:, 4:],
            local_signs[0][:, None, None],
            local_speeds[0][:, None, None],
        )
        along_columns = upwind(
            centre,
            jnp.roll(centre, 1, 2),
            jnp.roll(centre, 2, 2),
            jnp.roll(centre, -1, 2),
            jnp.roll(centre, -2, 2),
            local_signs[1][:, None, None],
            local_speeds[1][:, None, None],
        )
        advected = (centre - along_rows - along_columns).astype(jnp.bfloat16)
        current = lax.all_to_all(
            rotate_block(
                lax.all_to_all(advected, "ao", split_axis=2, concat_axis=0, tiled=True),
                kernel,
                turn_matrix,
            ),
            "ao",
            split_axis=0,
            concat_axis=2,
            tiled=True,
        )
    return current


LANES = 128
REACH = 2 * TIME_STEPS
GROUP = 8
SLOT = LANES // GROUP


def pack_kernel(place, main_ref, before_ref, after_ref, out_ref, main, sides):
    orients, rows, _ = main_ref.shape
    lane = lax.broadcasted_iota(jnp.int32, (orients, LANES), 1)
    main[...] = main_ref[...].astype(jnp.float32).reshape(orients * rows, LANES)
    wide_lane = lax.broadcasted_iota(jnp.int32, (orients * rows, LANES), 1)
    sides[...] = jnp.where(
        wide_lane < LANES // 2,
        after_ref[...].astype(jnp.float32).reshape(orients * rows, LANES),
        before_ref[...].astype(jnp.float32).reshape(orients * rows, LANES),
    )
    owner = ((lane + SLOT // 2) % LANES) // SLOT
    for group in range(rows // GROUP):
        packed = jnp.zeros((orients, LANES), jnp.float32)
        for slot in range(GROUP):
            row = group * GROUP + slot
            out_ref[1 + row] = main[pl.ds(row, orients, stride=rows), :].astype(jnp.bfloat16)
            edge = pltpu.roll(sides[pl.ds(row, orients, stride=rows), :], SLOT * slot, 1)
            packed = jnp.where(owner == slot, edge, packed)
        out_ref[0 if group == 0 else rows + 1] = packed.astype(jnp.bfloat16)


def pack(density, place, shift, part, devices, parts):
    share, rows, columns = density.shape
    tiles = columns // LANES
    step = share

    def tile(offset):
        def index(block, place_ref):
            target = lax.rem(place_ref[0] + shift, devices)
            return block, 0, lax.rem(target * parts + part + offset + tiles, tiles)

        return pl.BlockSpec((step, rows, LANES), index)

    return pl.pallas_call(
        pack_kernel,
        grid_spec=pltpu.PrefetchScalarGridSpec(
            num_scalar_prefetch=1,
            grid=(share // step,),
            in_specs=[tile(0), tile(-1), tile(1)],
            out_specs=pl.BlockSpec((rows + 2, step, LANES), lambda block, place_ref: (0, block, 0)),
            scratch_shapes=[pltpu.VMEM((step * rows, LANES), jnp.float32)] * 2,
        ),
        out_shape=jax.ShapeDtypeStruct((rows + 2, share, LANES), jnp.bfloat16),
        name="pack",
    )(place, density, density, density)


def unpack_kernel(devices, part, parts, place, *refs):
    blocks, out_ref, wide, staged, sems = refs[:devices], *refs[-4:]
    rows, share, _ = blocks[0].shape
    copies = []
    for shift in range(devices):
        wide[...] = blocks[shift][...].astype(jnp.float32).reshape(rows * share, LANES)
        for orient in range(share):
            staged[shift, orient] = wide[pl.ds(orient, rows, stride=share), :].astype(jnp.bfloat16)
        tile = lax.rem(place[0] + shift, devices) * parts + part
        copies.append(
            pltpu.make_async_copy(
                staged.at[shift],
                out_ref.at[:, :, pl.ds(pl.multiple_of(tile * LANES, LANES), LANES)],
                sems.at[shift],
            )
        )
        copies[-1].start()
    for copy in copies:
        copy.wait()


def unpack(blocks, place, part, parts, shape, before):
    devices = len(blocks)
    rows, share, _ = blocks[0].shape
    earlier = () if before is None else (before,)
    return pl.pallas_call(
        functools.partial(unpack_kernel, devices, part, parts),
        in_specs=[pl.BlockSpec(memory_space=pltpu.SMEM)]
        + [pl.BlockSpec(memory_space=pltpu.VMEM)] * devices
        + [pl.BlockSpec(memory_space=pl.ANY)] * len(earlier),
        out_specs=pl.BlockSpec(memory_space=pl.ANY),
        scratch_shapes=[
            pltpu.VMEM((rows * share, LANES), jnp.float32),
            pltpu.VMEM((devices, share, rows, LANES), jnp.bfloat16),
            pltpu.SemaphoreType.DMA((devices,)),
        ],
        out_shape=jax.ShapeDtypeStruct(shape, jnp.bfloat16),
        input_output_aliases={1 + devices: 0} if earlier else {},
        compiler_params=pltpu.CompilerParams(vmem_limit_bytes=16 * 2**20),
        name="unpack",
    )(place, *blocks, *earlier)


def steps_kernel(devices, *refs):
    blocks = refs[:devices]
    above, below, kernel, turn, coefficients = refs[devices : devices + 5]
    outs = refs[devices + 5 : 2 * devices + 5]
    buffers = refs[2 * devices + 5 : 2 * devices + 7]
    waiting = refs[2 * devices + 7 :]
    share = blocks[0].shape[1]
    number = share * devices
    rows = outs[0].shape[0]
    tiles = number // LANES

    def transposed(value_of):
        return jnp.concatenate([value_of(part).astype(jnp.float32) for part in range(devices)], 0).T

    def piece(ref, index, part):
        return ref[index, part * share : (part + 1) * share]

    def fill(first, last, value_of):
        for row in range(first, last):
            cells = transposed(lambda part: value_of(row, part))
            for tile in range(tiles):
                buffers[0][row + REACH, tile, 2 * GROUP : 2 * GROUP + LANES] = cells[
                    :, tile * LANES : (tile + 1) * LANES
                ]

    def fill_sides(first, last, value_of):
        cells = transposed(value_of)
        for row in range(first, last):
            slot = row % GROUP
            left, right = (SLOT * slot - GROUP) % LANES, SLOT * slot
            for tile in range(tiles):
                lanes = slice(tile * LANES, (tile + 1) * LANES)
                buffers[0][row + REACH, tile, GROUP : 2 * GROUP] = cells[left : left + GROUP, lanes]
                buffers[0][row + REACH, tile, 2 * GROUP + LANES : 3 * GROUP + LANES] = cells[
                    right : right + GROUP, lanes
                ]

    fill(-REACH, 0, lambda row, part: piece(above, row + REACH, part))
    fill(0, rows, lambda row, part: blocks[part][1 + row])
    fill(rows, rows + REACH, lambda row, part: piece(below, 1 + row - rows, part))
    fill_sides(-REACH, 0, lambda part: piece(above, REACH, part))
    fill_sides(0, GROUP, lambda part: blocks[part][0])
    fill_sides(GROUP, rows, lambda part: blocks[part][rows + 1])
    fill_sides(rows, rows + REACH, lambda part: piece(below, 0, part))

    def advect(source, index, start, length, target):
        for tile in range(tiles):
            lanes = slice(tile * LANES, (tile + 1) * LANES)
            keep, by_row, by_column, row_sign, column_sign = (coefficients[k : k + 1, lanes] for k in range(5))
            forward_row = jnp.broadcast_to(row_sign, (length, LANES)) > 0
            forward_column = jnp.broadcast_to(column_sign, (length, LANES)) > 0
            for half in range(2):

                def at(row, column):
                    return source[index + half + row, tile, start + column : start + column + length]

                row_one = jnp.where(forward_row, at(-1, 0), at(1, 0))
                row_two = jnp.where(forward_row, at(-2, 0), at(2, 0))
                column_one = jnp.where(forward_column, at(0, -1), at(0, 1))
                column_two = jnp.where(forward_column, at(0, -2), at(0, 2))
                value = (
                    keep * at(0, 0)
                    + by_row * (row_one - 0.25 * row_two)
                    + by_column * (column_one - 0.25 * column_two)
                )
                target[half * length : (half + 1) * length, lanes] = value.astype(jnp.bfloat16)

    def rotate(values):
        potential = jnp.dot(values, kernel[...], preferred_element_type=jnp.float32)
        drifted = (values.astype(jnp.float32) * (1.0 + potential)).astype(jnp.bfloat16)
        turned = jnp.dot(drifted, turn[...], preferred_element_type=jnp.float32)
        return (values.astype(jnp.float32) + rotation_rate * turned).astype(jnp.bfloat16)

    for step in range(TIME_STEPS):
        source, target = buffers[step % 2], buffers[(step + 1) % 2]
        last = step == TIME_STEPS - 1
        start, length = (2 * GROUP, LANES) if last else (GROUP, LANES + 2 * GROUP)
        low, pairs = 2 * (step + 1), rows // 2 + REACH - 2 * (step + 1)

        def finish(slot, index):
            result = rotate(waiting[slot][: 2 * length]).astype(jnp.float32)
            for half in range(2):
                cells = result[half * length : (half + 1) * length]
                if last:
                    back = cells.T.astype(jnp.bfloat16)
                    for part in range(devices):
                        outs[part][index - REACH + half] = back[part * share : (part + 1) * share]
                else:
                    for tile in range(tiles):
                        target[index + half, tile, start : start + length] = cells[
                            :, tile * LANES : (tile + 1) * LANES
                        ]

        advect(source, low, start, length, waiting[0])

        @pl.loop(0, pairs // 2)
        def _(turn_index):
            index = low + 4 * turn_index
            advect(source, index + 2, start, length, waiting[1])
            finish(0, index)
            advect(source, jnp.minimum(index + 4, low + 2 * pairs - 2), start, length, waiting[0])
            finish(1, index + 2)


def three_steps(blocks, above, below, kernel, turn, coefficients):
    devices = len(blocks)
    rows, share, _ = blocks[0].shape
    rows -= 2
    number = share * devices
    cells = (rows + 2 * REACH) * LANES
    vmem = pl.BlockSpec(memory_space=pltpu.VMEM)
    operands = (*blocks, above, below, kernel, turn, coefficients)
    return pl.pallas_call(
        functools.partial(steps_kernel, devices),
        in_specs=[vmem] * len(operands),
        out_specs=[vmem] * devices,
        out_shape=[jax.ShapeDtypeStruct((rows, share, LANES), jnp.bfloat16)] * devices,
        scratch_shapes=[
            *[pltpu.VMEM((rows + 2 * REACH, number // LANES, LANES + 4 * GROUP, LANES), jnp.float32)] * 2,
            *[pltpu.VMEM((2 * (LANES + 2 * GROUP), number), jnp.bfloat16)] * 2,
        ],
        compiler_params=pltpu.CompilerParams(vmem_limit_bytes=48 * 2**20),
        cost_estimate=pl.CostEstimate(
            flops=12 * number * number * cells, bytes_accessed=8 * 2**20, transcendentals=0
        ),
        name="three_steps",
    )(*operands)


def blocked(density, kernel, neighbours, weights, signs, speeds):
    devices = lax.axis_size("ao")
    share, rows, columns = density.shape
    parts = columns // devices // LANES
    here = lax.axis_index("ao")
    place = here.astype(jnp.int32).reshape(1)

    packed = [[pack(density, place, shift, part, devices, parts) for shift in range(devices)] for part in range(parts)]

    def turned(value, dim):
        pieces = [
            lax.dynamic_slice_in_dim(value, lax.rem(here - shift + devices, devices) * share, share, dim)
            for shift in range(devices)
        ]
        return jnp.concatenate(pieces, dim)

    turn = turned(turned(stencil_matrix(neighbours, weights), 0), 1)
    kernel = turned(turned(kernel, 0), 1)
    signs, speeds = turned(signs, 1), turned(speeds, 1)

    coefficients = jnp.stack(
        [
            1.0 - 1.5 * (speeds[0] + speeds[1]),
            2.0 * speeds[0],
            2.0 * speeds[1],
            (signs[0] == 1).astype(jnp.float32),
            (signs[1] == 1).astype(jnp.float32),
        ]
    )
    kernel, turn = kernel.T, turn.T

    size = lax.axis_size("gx")
    up = [(i, (i + 1) % size) for i in range(size)]
    down = [(j, i) for i, j in up]
    def ahead(value, shift):
        return lax.ppermute(value, "ao", [(i, (i + shift) % devices) for i in range(devices)])

    def after(value, *earlier):
        return lax.optimization_barrier((value, *earlier))[0]

    received = []
    for part in range(parts):
        blocks = packed[part]
        if received:
            earlier = received[-1]
            blocks = [after(block, early) for block, early in zip(blocks, earlier)]
        received.append([blocks[0]] + [ahead(blocks[shift], shift) for shift in range(1, devices)])
    results = []
    for part in range(parts):
        arrived = received[part]
        edges = [after(block, results[-1]) for block in arrived] if results else arrived
        above = lax.ppermute(jnp.concatenate([block[-(REACH + 1) :] for block in edges], 1), "gx", up)
        below = lax.ppermute(jnp.concatenate([block[: REACH + 1] for block in edges], 1), "gx", down)
        results.append(three_steps(arrived, above, below, kernel, turn, coefficients))
    evolved = None
    for part in range(parts):
        result = results[part]
        returned = [result[0]] + [ahead(result[shift], devices - shift) for shift in range(1, devices)]
        evolved = unpack(returned, place, part, parts, density.shape, evolved)
    return evolved


def solution(mesh):
    in_specs = (P("ao", "gx", None), P(), P(), P(), P(), P())
    out_specs = P("ao", "gx", None)

    def run(density, *rest):
        share, rows, columns = (
            density.shape[0] // mesh.shape["ao"],
            density.shape[1] // mesh.shape["gx"],
            density.shape[2] // mesh.shape["ao"],
        )
        fits = columns % LANES == 0 and share % 32 == 0 and rows == 2 * GROUP
        body = jax.shard_map(
            blocked if fits else per_device, mesh=mesh, in_specs=in_specs, out_specs=out_specs, check_vma=False
        )
        return body(density, *rest)

    return run
```

```python
import functools

import jax
import jax.numpy as jnp
from jax import lax
from jax.experimental import pallas as pl
from jax.experimental.pallas import tpu as pltpu
from jax.sharding import PartitionSpec as P

TIME_STEPS = 3


rotation_rate = 0.05


def extended(value, sides, width):
    for axis, dim in sides:
        devices, length = (lax.axis_size(axis), value.shape[dim])
        up = [(i, (i + 1) % devices) for i in range(devices)]
        down = [(j, i) for i, j in up]
        last = lax.slice_in_dim(value, length - width, length, axis=dim)
        leading = lax.slice_in_dim(value, 0, width, axis=dim)
        before = lax.ppermute(last, axis, up)
        after = lax.ppermute(leading, axis, down)
        value = jnp.concatenate([before, value, after], axis=dim)
    return value


def upwind(centre, behind_one, behind_two, ahead_one, ahead_two, direction, speed):
    rear = 0.5 * (3.0 * centre - 4.0 * behind_one + behind_two)
    front = 0.5 * (3.0 * centre - 4.0 * ahead_one + ahead_two)
    return speed * jnp.where(direction == 1, rear, front)


def stencil_matrix(neighbours, weights):
    number = neighbours.shape[0]
    labels = jnp.arange(number, dtype=jnp.int32)
    matches = (neighbours[:, :, None] == labels[None, None, :]).astype(jnp.float32)
    scaled = weights.astype(jnp.float32)
    coupled = jnp.sum(scaled[:, :, None] * matches, axis=1)
    totals = jnp.sum(scaled, axis=1)
    identity = (labels[:, None] == labels[None, :]).astype(jnp.float32)
    return (coupled - totals[:, None] * identity).astype(jnp.bfloat16)


def rotate_block(block, kernel, turn_matrix):
    block_shape = block.shape
    values = block.reshape(block_shape[0], -1)
    potential = jnp.dot(kernel, values, preferred_element_type=jnp.float32)
    wide_values = values.astype(jnp.float32)
    drifted = (wide_values * (1.0 + potential)).astype(jnp.bfloat16)
    turned = jnp.dot(turn_matrix, drifted, preferred_element_type=jnp.float32)
    return (wide_values + rotation_rate * turned).astype(jnp.bfloat16).reshape(block_shape)


def per_device(density, kernel, neighbours, weights, signs, speeds):
    turn_matrix = stencil_matrix(neighbours, weights)
    share = density.shape[0]
    offset = lax.axis_index("ao") * share
    local_signs = lax.dynamic_slice_in_dim(signs, offset, share, 1)
    local_speeds = lax.dynamic_slice_in_dim(speeds, offset, share, 1)
    current = density
    for section_index in range(TIME_STEPS):
        widened = extended(current, (("gx", 1),), 2).astype(jnp.float32)
        centre = current.astype(jnp.float32)
        along_rows = upwind(
            centre,
            widened[:, 1:-3],
            widened[:, :-4],
            widened[:, 3:-1],
            widened[:, 4:],
            local_signs[0][:, None, None],
            local_speeds[0][:, None, None],
        )
        along_columns = upwind(
            centre,
            jnp.roll(centre, 1, 2),
            jnp.roll(centre, 2, 2),
            jnp.roll(centre, -1, 2),
            jnp.roll(centre, -2, 2),
            local_signs[1][:, None, None],
            local_speeds[1][:, None, None],
        )
        advected = (centre - along_rows - along_columns).astype(jnp.bfloat16)
        current = lax.all_to_all(
            rotate_block(
                lax.all_to_all(advected, "ao", split_axis=2, concat_axis=0, tiled=True),
                kernel,
                turn_matrix,
            ),
            "ao",
            split_axis=0,
            concat_axis=2,
            tiled=True,
        )
    return current


LANES = 128
REACH = 2 * TIME_STEPS
GROUP = 8
SLOT = LANES // GROUP


def pack_kernel(place, main_ref, *refs):
    *side_refs, out_ref, main, sides = refs
    orients, rows, _ = main_ref.shape
    both = len(side_refs) == 2
    width = SLOT if both else GROUP
    slots = LANES // width
    lane = lax.broadcasted_iota(jnp.int32, (orients, LANES), 1)
    owner = ((lane + SLOT // 2) % LANES) // SLOT if both else lane // GROUP

    def flat(ref):
        return ref[...].astype(jnp.float32).reshape(orients * rows, LANES)

    main[...] = flat(main_ref)
    if both:
        wide_lane = lax.broadcasted_iota(jnp.int32, (orients * rows, LANES), 1)
        sides[...] = jnp.where(wide_lane < LANES // 2, flat(side_refs[0]), flat(side_refs[1]))
    else:
        sides[...] = flat(side_refs[0])
    for group in range(rows // slots):
        packed = jnp.zeros((orients, LANES), jnp.float32)
        for slot in range(slots):
            row = group * slots + slot
            out_ref[1 + row] = main[pl.ds(row, orients, stride=rows), :].astype(jnp.bfloat16)
            edge = pltpu.roll(sides[pl.ds(row, orients, stride=rows), :], width * slot, 1)
            packed = jnp.where(owner == slot, edge, packed)
        out_ref[0 if group == 0 else rows + 1] = packed.astype(jnp.bfloat16)


def pack(density, place, shift, part, devices, parts):
    share, rows, columns = density.shape
    tiles = columns // LANES
    offsets = (0, 1) if part else (0, 1, -1)
    length = rows + (1 if part else 2)

    def tile(offset):
        def index(block, place_ref):
            target = lax.rem(place_ref[0] + shift, devices)
            return block, 0, lax.rem(target * parts + part + offset + tiles, tiles)

        return pl.BlockSpec((share, rows, LANES), index)

    return pl.pallas_call(
        pack_kernel,
        grid_spec=pltpu.PrefetchScalarGridSpec(
            num_scalar_prefetch=1,
            grid=(1,),
            in_specs=[tile(offset) for offset in offsets],
            out_specs=pl.BlockSpec((length, share, LANES), lambda block, place_ref: (0, block, 0)),
            scratch_shapes=[pltpu.VMEM((share * rows, LANES), jnp.float32)] * 2,
        ),
        out_shape=jax.ShapeDtypeStruct((length, share, LANES), jnp.bfloat16),
        name="pack",
    )(place, *[density] * len(offsets))


def unpack_kernel(devices, part, parts, place, *refs):
    blocks, out_ref, wide, staged, sems = refs[:devices], *refs[-4:]
    rows, share, _ = blocks[0].shape
    copies = []
    for shift in range(devices):
        wide[...] = blocks[shift][...].astype(jnp.float32).reshape(rows * share, LANES)
        for orient in range(share):
            staged[shift, orient] = wide[pl.ds(orient, rows, stride=share), :].astype(jnp.bfloat16)
        tile = lax.rem(place[0] + shift, devices) * parts + part
        copies.append(
            pltpu.make_async_copy(
                staged.at[shift],
                out_ref.at[:, :, pl.ds(pl.multiple_of(tile * LANES, LANES), LANES)],
                sems.at[shift],
            )
        )
        copies[-1].start()
    for copy in copies:
        copy.wait()


def unpack(blocks, place, part, parts, shape, before):
    devices = len(blocks)
    rows, share, _ = blocks[0].shape
    earlier = () if before is None else (before,)
    return pl.pallas_call(
        functools.partial(unpack_kernel, devices, part, parts),
        in_specs=[pl.BlockSpec(memory_space=pltpu.SMEM)]
        + [pl.BlockSpec(memory_space=pltpu.VMEM)] * devices
        + [pl.BlockSpec(memory_space=pl.ANY)] * len(earlier),
        out_specs=pl.BlockSpec(memory_space=pl.ANY),
        scratch_shapes=[
            pltpu.VMEM((rows * share, LANES), jnp.float32),
            pltpu.VMEM((devices, share, rows, LANES), jnp.bfloat16),
            pltpu.SemaphoreType.DMA((devices,)),
        ],
        out_shape=jax.ShapeDtypeStruct(shape, jnp.bfloat16),
        input_output_aliases={1 + devices: 0} if earlier else {},
        compiler_params=pltpu.CompilerParams(vmem_limit_bytes=16 * 2**20),
        name="unpack",
    )(place, *blocks, *earlier)


def steps_kernel(devices, joined, followed, *refs):
    blocks, refs = refs[:devices], refs[devices:]
    above, below, kernel, turn, coefficients = refs[:5]
    edge_in, refs = (refs[5], refs[6:]) if joined else (None, refs[5:])
    outs, refs = refs[:devices], refs[devices:]
    edge_out, refs = (refs[0], refs[1:]) if followed else (None, refs)
    buffers, waiting = refs[:2], refs[2:]
    share = blocks[0].shape[1]
    number = share * devices
    rows = outs[0].shape[0]
    tiles = number // LANES

    def transposed(value_of):
        return jnp.concatenate([value_of(part).astype(jnp.float32) for part in range(devices)], 0).T

    def piece(ref, index, part):
        return ref[index, part * share : (part + 1) * share]

    def fill(first, last, value_of):
        for row in range(first, last):
            cells = transposed(lambda part: value_of(row, part))
            for tile in range(tiles):
                lanes = slice(tile * LANES, (tile + 1) * LANES)
                buffers[0][row + REACH, tile, 2 * GROUP : 2 * GROUP + LANES] = cells[:, lanes]
                if followed:
                    edge_out[row + REACH, tile] = cells[LANES - GROUP :, lanes]

    def fill_sides(first, last, value_of):
        cells = transposed(value_of)
        for row in range(first, last):
            if joined:
                right = GROUP * (row % rows)
            else:
                right = SLOT * (row % GROUP)
                left = (right - GROUP) % LANES
            for tile in range(tiles):
                lanes = slice(tile * LANES, (tile + 1) * LANES)
                buffers[0][row + REACH, tile, GROUP : 2 * GROUP] = (
                    edge_in[row + REACH, tile] if joined else cells[left : left + GROUP, lanes]
                )
                buffers[0][row + REACH, tile, 2 * GROUP + LANES : 3 * GROUP + LANES] = cells[
                    right : right + GROUP, lanes
                ]

    lead = REACH + 1 if joined else REACH
    fill(-REACH, 0, lambda row, part: piece(above, row + lead, part))
    fill(0, rows, lambda row, part: blocks[part][1 + row])
    fill(rows, rows + REACH, lambda row, part: piece(below, 1 + row - rows, part))
    fill_sides(-REACH, 0, lambda part: piece(above, 0 if joined else REACH, part))
    if joined:
        fill_sides(0, rows, lambda part: blocks[part][0])
    else:
        fill_sides(0, GROUP, lambda part: blocks[part][0])
        fill_sides(GROUP, rows, lambda part: blocks[part][rows + 1])
    fill_sides(rows, rows + REACH, lambda part: piece(below, 0, part))

    def advect(source, index, start, length, target):
        for tile in range(tiles):
            lanes = slice(tile * LANES, (tile + 1) * LANES)
            keep, by_row, by_column, row_sign, column_sign = (coefficients[k : k + 1, lanes] for k in range(5))
            forward_row = jnp.broadcast_to(row_sign, (length, LANES)) > 0
            forward_column = jnp.broadcast_to(column_sign, (length, LANES)) > 0
            for half in range(2):

                def at(row, column):
                    return source[index + half + row, tile, start + column : start + column + length]

                row_one = jnp.where(forward_row, at(-1, 0), at(1, 0))
                row_two = jnp.where(forward_row, at(-2, 0), at(2, 0))
                column_one = jnp.where(forward_column, at(0, -1), at(0, 1))
                column_two = jnp.where(forward_column, at(0, -2), at(0, 2))
                value = (
                    keep * at(0, 0)
                    + by_row * (row_one - 0.25 * row_two)
                    + by_column * (column_one - 0.25 * column_two)
                )
                target[half * length : (half + 1) * length, lanes] = value.astype(jnp.bfloat16)

    def rotate(values):
        potential = jnp.dot(values, kernel[...], preferred_element_type=jnp.float32)
        drifted = (values.astype(jnp.float32) * (1.0 + potential)).astype(jnp.bfloat16)
        turned = jnp.dot(drifted, turn[...], preferred_element_type=jnp.float32)
        return (values.astype(jnp.float32) + rotation_rate * turned).astype(jnp.bfloat16)

    for step in range(TIME_STEPS):
        source, target = buffers[step % 2], buffers[(step + 1) % 2]
        last = step == TIME_STEPS - 1
        start, length = (2 * GROUP, LANES) if last else (GROUP, LANES + 2 * GROUP)
        low, pairs = 2 * (step + 1), rows // 2 + REACH - 2 * (step + 1)

        def finish(slot, index):
            result = rotate(waiting[slot][: 2 * length]).astype(jnp.float32)
            for half in range(2):
                cells = result[half * length : (half + 1) * length]
                if last:
                    back = cells.T.astype(jnp.bfloat16)
                    for part in range(devices):
                        outs[part][index - REACH + half] = back[part * share : (part + 1) * share]
                else:
                    for tile in range(tiles):
                        target[index + half, tile, start : start + length] = cells[
                            :, tile * LANES : (tile + 1) * LANES
                        ]

        advect(source, low, start, length, waiting[0])

        @pl.loop(0, pairs // 2)
        def _(turn_index):
            index = low + 4 * turn_index
            advect(source, index + 2, start, length, waiting[1])
            finish(0, index)
            advect(source, jnp.minimum(index + 4, low + 2 * pairs - 2), start, length, waiting[0])
            finish(1, index + 2)


def three_steps(blocks, above, below, kernel, turn, coefficients, rows, edge, followed):
    devices = len(blocks)
    share = blocks[0].shape[1]
    number = share * devices
    tiles = number // LANES
    tall = rows + 2 * REACH
    vmem = pl.BlockSpec(memory_space=pltpu.VMEM)
    operands = (*blocks, above, below, kernel, turn, coefficients, *([] if edge is None else [edge]))
    out_shape = [jax.ShapeDtypeStruct((rows, share, LANES), jnp.bfloat16)] * devices
    if followed:
        out_shape.append(jax.ShapeDtypeStruct((tall, tiles, GROUP, LANES), jnp.float32))
    outs = pl.pallas_call(
        functools.partial(steps_kernel, devices, edge is not None, followed),
        in_specs=[vmem] * len(operands),
        out_specs=[vmem] * len(out_shape),
        out_shape=out_shape,
        scratch_shapes=[
            *[pltpu.VMEM((tall, tiles, LANES + 4 * GROUP, LANES), jnp.float32)] * 2,
            *[pltpu.VMEM((2 * (LANES + 2 * GROUP), number), jnp.bfloat16)] * 2,
        ],
        compiler_params=pltpu.CompilerParams(vmem_limit_bytes=48 * 2**20),
        cost_estimate=pl.CostEstimate(
            flops=12 * number * number * tall * LANES, bytes_accessed=8 * 2**20, transcendentals=0
        ),
        name="three_steps",
    )(*operands)
    return outs[:devices], outs[devices] if followed else None


def blocked(density, kernel, neighbours, weights, signs, speeds):
    devices = lax.axis_size("ao")
    share, rows, columns = density.shape
    parts = columns // devices // LANES
    here = lax.axis_index("ao")
    place = here.astype(jnp.int32).reshape(1)

    packed = [[pack(density, place, shift, part, devices, parts) for shift in range(devices)] for part in range(parts)]

    def turned(value, dim):
        pieces = [
            lax.dynamic_slice_in_dim(value, lax.rem(here - shift + devices, devices) * share, share, dim)
            for shift in range(devices)
        ]
        return jnp.concatenate(pieces, dim)

    turn = turned(turned(stencil_matrix(neighbours, weights), 0), 1)
    kernel = turned(turned(kernel, 0), 1)
    signs, speeds = turned(signs, 1), turned(speeds, 1)

    coefficients = jnp.stack(
        [
            1.0 - 1.5 * (speeds[0] + speeds[1]),
            2.0 * speeds[0],
            2.0 * speeds[1],
            (signs[0] == 1).astype(jnp.float32),
            (signs[1] == 1).astype(jnp.float32),
        ]
    )
    kernel, turn = kernel.T, turn.T

    size = lax.axis_size("gx")
    up = [(i, (i + 1) % size) for i in range(size)]
    down = [(j, i) for i, j in up]
    def ahead(value, shift):
        return lax.ppermute(value, "ao", [(i, (i + shift) % devices) for i in range(devices)])

    def after(value, *earlier):
        return lax.optimization_barrier((value, *earlier))[0]

    received = []
    for part in range(parts):
        blocks = packed[part]
        if received:
            earlier = received[-1]
            blocks = [after(block, early) for block, early in zip(blocks, earlier)]
        received.append([blocks[0]] + [ahead(blocks[shift], shift) for shift in range(1, devices)])
    results, edge = [], None
    for part in range(parts):
        arrived = received[part]
        ends = [after(block, results[-1]) for block in arrived] if results else arrived

        def joint(first, last):
            return jnp.concatenate([block[first:last] for block in ends], 1)

        length = ends[0].shape[0]
        if part:
            upper = jnp.concatenate([joint(0, 1), joint(length - REACH, length)], 0)
        else:
            upper = joint(length - REACH - 1, length)
        above = lax.ppermute(upper, "gx", up)
        below = lax.ppermute(joint(0, REACH + 1), "gx", down)
        result, edge = three_steps(
            arrived, above, below, kernel, turn, coefficients, rows, edge, part + 1 < parts
        )
        results.append(result)
    evolved = None
    for part in range(parts):
        result = results[part]
        returned = [result[0]] + [ahead(result[shift], devices - shift) for shift in range(1, devices)]
        evolved = unpack(returned, place, part, parts, density.shape, evolved)
    return evolved


def solution(mesh):
    in_specs = (P("ao", "gx", None), P(), P(), P(), P(), P())
    out_specs = P("ao", "gx", None)

    def run(density, *rest):
        share, rows, columns = (
            density.shape[0] // mesh.shape["ao"],
            density.shape[1] // mesh.shape["gx"],
            density.shape[2] // mesh.shape["ao"],
        )
        fits = columns % LANES == 0 and share % 32 == 0 and rows == 2 * GROUP
        body = jax.shard_map(
            blocked if fits else per_device, mesh=mesh, in_specs=in_specs, out_specs=out_specs, check_vma=False
        )
        return body(density, *rest)

    return run
```

```python
import functools

import jax
import jax.numpy as jnp
from jax import lax
from jax.experimental import pallas as pl
from jax.experimental.pallas import tpu as pltpu
from jax.sharding import PartitionSpec as P

TIME_STEPS = 3


rotation_rate = 0.05


def extended(value, sides, width):
    for axis, dim in sides:
        devices, length = (lax.axis_size(axis), value.shape[dim])
        up = [(i, (i + 1) % devices) for i in range(devices)]
        down = [(j, i) for i, j in up]
        last = lax.slice_in_dim(value, length - width, length, axis=dim)
        leading = lax.slice_in_dim(value, 0, width, axis=dim)
        before = lax.ppermute(last, axis, up)
        after = lax.ppermute(leading, axis, down)
        value = jnp.concatenate([before, value, after], axis=dim)
    return value


def upwind(centre, behind_one, behind_two, ahead_one, ahead_two, direction, speed):
    rear = 0.5 * (3.0 * centre - 4.0 * behind_one + behind_two)
    front = 0.5 * (3.0 * centre - 4.0 * ahead_one + ahead_two)
    return speed * jnp.where(direction == 1, rear, front)


def stencil_matrix(neighbours, weights):
    number = neighbours.shape[0]
    labels = jnp.arange(number, dtype=jnp.int32)
    matches = (neighbours[:, :, None] == labels[None, None, :]).astype(jnp.float32)
    scaled = weights.astype(jnp.float32)
    coupled = jnp.sum(scaled[:, :, None] * matches, axis=1)
    totals = jnp.sum(scaled, axis=1)
    identity = (labels[:, None] == labels[None, :]).astype(jnp.float32)
    return (coupled - totals[:, None] * identity).astype(jnp.bfloat16)


def rotate_block(block, kernel, turn_matrix):
    block_shape = block.shape
    values = block.reshape(block_shape[0], -1)
    potential = jnp.dot(kernel, values, preferred_element_type=jnp.float32)
    wide_values = values.astype(jnp.float32)
    drifted = (wide_values * (1.0 + potential)).astype(jnp.bfloat16)
    turned = jnp.dot(turn_matrix, drifted, preferred_element_type=jnp.float32)
    return (wide_values + rotation_rate * turned).astype(jnp.bfloat16).reshape(block_shape)


def per_device(density, kernel, neighbours, weights, signs, speeds):
    turn_matrix = stencil_matrix(neighbours, weights)
    share = density.shape[0]
    offset = lax.axis_index("ao") * share
    local_signs = lax.dynamic_slice_in_dim(signs, offset, share, 1)
    local_speeds = lax.dynamic_slice_in_dim(speeds, offset, share, 1)
    current = density
    for section_index in range(TIME_STEPS):
        widened = extended(current, (("gx", 1),), 2).astype(jnp.float32)
        centre = current.astype(jnp.float32)
        along_rows = upwind(
            centre,
            widened[:, 1:-3],
            widened[:, :-4],
            widened[:, 3:-1],
            widened[:, 4:],
            local_signs[0][:, None, None],
            local_speeds[0][:, None, None],
        )
        along_columns = upwind(
            centre,
            jnp.roll(centre, 1, 2),
            jnp.roll(centre, 2, 2),
            jnp.roll(centre, -1, 2),
            jnp.roll(centre, -2, 2),
            local_signs[1][:, None, None],
            local_speeds[1][:, None, None],
        )
        advected = (centre - along_rows - along_columns).astype(jnp.bfloat16)
        current = lax.all_to_all(
            rotate_block(
                lax.all_to_all(advected, "ao", split_axis=2, concat_axis=0, tiled=True),
                kernel,
                turn_matrix,
            ),
            "ao",
            split_axis=0,
            concat_axis=2,
            tiled=True,
        )
    return current


LANES = 128
REACH = 2 * TIME_STEPS
GROUP = 8
SLOT = LANES // GROUP
TOGETHER = 4


def pack_kernel(place, main_ref, *refs):
    *side_refs, out_ref, main, sides = refs
    orients, rows, _ = main_ref.shape
    both = len(side_refs) == 2
    width = SLOT if both else GROUP
    slots = LANES // width
    lane = lax.broadcasted_iota(jnp.int32, (orients, LANES), 1)
    owner = ((lane + SLOT // 2) % LANES) // SLOT if both else lane // GROUP

    def flat(ref):
        return ref[...].astype(jnp.float32).reshape(orients * rows, LANES)

    main[...] = flat(main_ref)
    if both:
        wide_lane = lax.broadcasted_iota(jnp.int32, (orients * rows, LANES), 1)
        sides[...] = jnp.where(wide_lane < LANES // 2, flat(side_refs[0]), flat(side_refs[1]))
    else:
        sides[...] = flat(side_refs[0])
    for group in range(rows // slots):
        packed = jnp.zeros((orients, LANES), jnp.float32)
        for slot in range(slots):
            row = group * slots + slot
            out_ref[1 + row] = main[pl.ds(row, orients, stride=rows), :].astype(jnp.bfloat16)
            edge = pltpu.roll(sides[pl.ds(row, orients, stride=rows), :], width * slot, 1)
            packed = jnp.where(owner == slot, edge, packed)
        out_ref[0 if group == 0 else rows + 1] = packed.astype(jnp.bfloat16)


def pack(density, place, shift, part, devices, parts):
    share, rows, columns = density.shape
    tiles = columns // LANES
    offsets = (0, 1) if part else (0, 1, -1)
    length = rows + (1 if part else 2)

    def tile(offset):
        def index(block, place_ref):
            target = lax.rem(place_ref[0] + shift, devices)
            return block, 0, lax.rem(target * parts + part + offset + tiles, tiles)

        return pl.BlockSpec((share, rows, LANES), index)

    return pl.pallas_call(
        pack_kernel,
        grid_spec=pltpu.PrefetchScalarGridSpec(
            num_scalar_prefetch=1,
            grid=(1,),
            in_specs=[tile(offset) for offset in offsets],
            out_specs=pl.BlockSpec((length, share, LANES), lambda block, place_ref: (0, block, 0)),
            scratch_shapes=[pltpu.VMEM((share * rows, LANES), jnp.float32)] * 2,
        ),
        out_shape=jax.ShapeDtypeStruct((length, share, LANES), jnp.bfloat16),
        name="pack",
    )(place, *[density] * len(offsets))


def unpack_kernel(devices, part, parts, place, *refs):
    blocks, out_ref, wide, staged, sems = refs[:devices], *refs[-4:]
    rows, share, _ = blocks[0].shape
    copies = []
    for shift in range(devices):
        wide[...] = blocks[shift][...].astype(jnp.float32).reshape(rows * share, LANES)
        for orient in range(share):
            staged[shift, orient] = wide[pl.ds(orient, rows, stride=share), :].astype(jnp.bfloat16)
        tile = lax.rem(place[0] + shift, devices) * parts + part
        copies.append(
            pltpu.make_async_copy(
                staged.at[shift],
                out_ref.at[:, :, pl.ds(pl.multiple_of(tile * LANES, LANES), LANES)],
                sems.at[shift],
            )
        )
        copies[-1].start()
    for copy in copies:
        copy.wait()


def unpack(blocks, place, part, parts, shape, before):
    devices = len(blocks)
    rows, share, _ = blocks[0].shape
    earlier = () if before is None else (before,)
    return pl.pallas_call(
        functools.partial(unpack_kernel, devices, part, parts),
        in_specs=[pl.BlockSpec(memory_space=pltpu.SMEM)]
        + [pl.BlockSpec(memory_space=pltpu.VMEM)] * devices
        + [pl.BlockSpec(memory_space=pl.ANY)] * len(earlier),
        out_specs=pl.BlockSpec(memory_space=pl.ANY),
        scratch_shapes=[
            pltpu.VMEM((rows * share, LANES), jnp.float32),
            pltpu.VMEM((devices, share, rows, LANES), jnp.bfloat16),
            pltpu.SemaphoreType.DMA((devices,)),
        ],
        out_shape=jax.ShapeDtypeStruct(shape, jnp.bfloat16),
        input_output_aliases={1 + devices: 0} if earlier else {},
        compiler_params=pltpu.CompilerParams(vmem_limit_bytes=16 * 2**20),
        name="unpack",
    )(place, *blocks, *earlier)


def steps_kernel(devices, joined, followed, *refs):
    blocks, refs = refs[:devices], refs[devices:]
    above, below, kernel, turn, coefficients = refs[:5]
    edge_in, refs = (refs[5], refs[6:]) if joined else (None, refs[5:])
    outs, refs = refs[:devices], refs[devices:]
    edge_out, refs = (refs[0], refs[1:]) if followed else (None, refs)
    buffers, waiting = refs[:2], refs[2]
    together = waiting.shape[1] // (LANES + 2 * GROUP)
    share = blocks[0].shape[1]
    number = share * devices
    rows = outs[0].shape[0]
    tiles = number // LANES

    def transposed(value_of):
        return jnp.concatenate([value_of(part).astype(jnp.float32) for part in range(devices)], 0).T

    def piece(ref, index, part):
        return ref[index, part * share : (part + 1) * share]

    def fill(first, last, value_of):
        for row in range(first, last):
            cells = transposed(lambda part: value_of(row, part))
            for tile in range(tiles):
                lanes = slice(tile * LANES, (tile + 1) * LANES)
                buffers[0][row + REACH, tile, 2 * GROUP : 2 * GROUP + LANES] = cells[:, lanes]
                if followed:
                    edge_out[row + REACH, tile] = cells[LANES - GROUP :, lanes]

    def fill_sides(first, last, value_of):
        cells = transposed(value_of)
        for row in range(first, last):
            if joined:
                right = GROUP * (row % rows)
            else:
                right = SLOT * (row % GROUP)
                left = (right - GROUP) % LANES
            for tile in range(tiles):
                lanes = slice(tile * LANES, (tile + 1) * LANES)
                buffers[0][row + REACH, tile, GROUP : 2 * GROUP] = (
                    edge_in[row + REACH, tile] if joined else cells[left : left + GROUP, lanes]
                )
                buffers[0][row + REACH, tile, 2 * GROUP + LANES : 3 * GROUP + LANES] = cells[
                    right : right + GROUP, lanes
                ]

    lead = REACH + 1 if joined else REACH
    fill(-REACH, 0, lambda row, part: piece(above, row + lead, part))
    fill(0, rows, lambda row, part: blocks[part][1 + row])
    fill(rows, rows + REACH, lambda row, part: piece(below, 1 + row - rows, part))
    fill_sides(-REACH, 0, lambda part: piece(above, 0 if joined else REACH, part))
    if joined:
        fill_sides(0, rows, lambda part: blocks[part][0])
    else:
        fill_sides(0, GROUP, lambda part: blocks[part][0])
        fill_sides(GROUP, rows, lambda part: blocks[part][rows + 1])
    fill_sides(rows, rows + REACH, lambda part: piece(below, 0, part))

    def advect(source, index, start, length, target):
        for tile in range(tiles):
            lanes = slice(tile * LANES, (tile + 1) * LANES)
            keep, by_row, by_column, row_sign, column_sign = (coefficients[k : k + 1, lanes] for k in range(5))
            forward_row = jnp.broadcast_to(row_sign, (length, LANES)) > 0
            forward_column = jnp.broadcast_to(column_sign, (length, LANES)) > 0
            for half in range(together):

                def at(row, column):
                    return source[index + half + row, tile, start + column : start + column + length]

                row_one = jnp.where(forward_row, at(-1, 0), at(1, 0))
                row_two = jnp.where(forward_row, at(-2, 0), at(2, 0))
                column_one = jnp.where(forward_column, at(0, -1), at(0, 1))
                column_two = jnp.where(forward_column, at(0, -2), at(0, 2))
                value = (
                    keep * at(0, 0)
                    + by_row * (row_one - 0.25 * row_two)
                    + by_column * (column_one - 0.25 * column_two)
                )
                target[half * length : (half + 1) * length, lanes] = value.astype(jnp.bfloat16)

    def rotate(values):
        potential = jnp.dot(values, kernel[...], preferred_element_type=jnp.float32)
        drifted = (values.astype(jnp.float32) * (1.0 + potential)).astype(jnp.bfloat16)
        turned = jnp.dot(drifted, turn[...], preferred_element_type=jnp.float32)
        return (values.astype(jnp.float32) + rotation_rate * turned).astype(jnp.bfloat16)

    for step in range(TIME_STEPS):
        source, target = buffers[step % 2], buffers[(step + 1) % 2]
        last = step == TIME_STEPS - 1
        start, length = (2 * GROUP, LANES) if last else (GROUP, LANES + 2 * GROUP)
        low = 2 * (step + 1)
        turns = (rows + 2 * REACH - 2 * low) // together

        def finish(slot, index):
            result = rotate(waiting[slot, : together * length]).astype(jnp.float32)
            for half in range(together):
                cells = result[half * length : (half + 1) * length]
                if last:
                    back = cells.T.astype(jnp.bfloat16)
                    for part in range(devices):
                        outs[part][index - REACH + half] = back[part * share : (part + 1) * share]
                else:
                    for tile in range(tiles):
                        target[index + half, tile, start : start + length] = cells[
                            :, tile * LANES : (tile + 1) * LANES
                        ]

        advect(source, low, start, length, waiting.at[0])

        @pl.loop(0, turns)
        def _(turn_index):
            index = low + together * turn_index
            slot = lax.rem(turn_index, 2)
            following = jnp.minimum(index + together, low + together * (turns - 1))
            advect(source, following, start, length, waiting.at[1 - slot])
            finish(slot, index)


def three_steps(blocks, above, below, kernel, turn, coefficients, rows, edge, followed):
    devices = len(blocks)
    share = blocks[0].shape[1]
    number = share * devices
    tiles = number // LANES
    tall = rows + 2 * REACH
    vmem = pl.BlockSpec(memory_space=pltpu.VMEM)
    operands = (*blocks, above, below, kernel, turn, coefficients, *([] if edge is None else [edge]))
    out_shape = [jax.ShapeDtypeStruct((rows, share, LANES), jnp.bfloat16)] * devices
    if followed:
        out_shape.append(jax.ShapeDtypeStruct((tall, tiles, GROUP, LANES), jnp.float32))
    outs = pl.pallas_call(
        functools.partial(steps_kernel, devices, edge is not None, followed),
        in_specs=[vmem] * len(operands),
        out_specs=[vmem] * len(out_shape),
        out_shape=out_shape,
        scratch_shapes=[
            *[pltpu.VMEM((tall, tiles, LANES + 4 * GROUP, LANES), jnp.float32)] * 2,
            pltpu.VMEM((2, TOGETHER * (LANES + 2 * GROUP), number), jnp.bfloat16),
        ],
        compiler_params=pltpu.CompilerParams(vmem_limit_bytes=48 * 2**20),
        cost_estimate=pl.CostEstimate(
            flops=12 * number * number * tall * LANES, bytes_accessed=8 * 2**20, transcendentals=0
        ),
        name="three_steps",
    )(*operands)
    return outs[:devices], outs[devices] if followed else None


def blocked(density, kernel, neighbours, weights, signs, speeds):
    devices = lax.axis_size("ao")
    share, rows, columns = density.shape
    parts = columns // devices // LANES
    here = lax.axis_index("ao")
    place = here.astype(jnp.int32).reshape(1)

    packed = [[pack(density, place, shift, part, devices, parts) for shift in range(devices)] for part in range(parts)]

    def turned(value, dim):
        pieces = [
            lax.dynamic_slice_in_dim(value, lax.rem(here - shift + devices, devices) * share, share, dim)
            for shift in range(devices)
        ]
        return jnp.concatenate(pieces, dim)

    turn = turned(turned(stencil_matrix(neighbours, weights), 0), 1)
    kernel = turned(turned(kernel, 0), 1)
    signs, speeds = turned(signs, 1), turned(speeds, 1)

    coefficients = jnp.stack(
        [
            1.0 - 1.5 * (speeds[0] + speeds[1]),
            2.0 * speeds[0],
            2.0 * speeds[1],
            (signs[0] == 1).astype(jnp.float32),
            (signs[1] == 1).astype(jnp.float32),
        ]
    )
    kernel, turn = kernel.T, turn.T

    size = lax.axis_size("gx")
    up = [(i, (i + 1) % size) for i in range(size)]
    down = [(j, i) for i, j in up]
    def ahead(value, shift):
        return lax.ppermute(value, "ao", [(i, (i + shift) % devices) for i in range(devices)])

    def after(value, *earlier):
        return lax.optimization_barrier((value, *earlier))[0]

    received = []
    for part in range(parts):
        blocks = packed[part]
        if received:
            earlier = received[-1]
            blocks = [after(block, early) for block, early in zip(blocks, earlier)]
        received.append([blocks[0]] + [ahead(blocks[shift], shift) for shift in range(1, devices)])
    results, edge = [], None
    for part in range(parts):
        arrived = received[part]
        ends = [after(block, results[-1]) for block in arrived] if results else arrived

        def joint(first, last):
            return jnp.concatenate([block[first:last] for block in ends], 1)

        length = ends[0].shape[0]
        if part:
            upper = jnp.concatenate([joint(0, 1), joint(length - REACH, length)], 0)
        else:
            upper = joint(length - REACH - 1, length)
        above = lax.ppermute(upper, "gx", up)
        below = lax.ppermute(joint(0, REACH + 1), "gx", down)
        result, edge = three_steps(
            arrived, above, below, kernel, turn, coefficients, rows, edge, part + 1 < parts
        )
        results.append(result)
    evolved = None
    for part in range(parts):
        result = results[part]
        returned = [result[0]] + [ahead(result[shift], devices - shift) for shift in range(1, devices)]
        evolved = unpack(returned, place, part, parts, density.shape, evolved)
    return evolved


def solution(mesh):
    in_specs = (P("ao", "gx", None), P(), P(), P(), P(), P())
    out_specs = P("ao", "gx", None)

    def run(density, *rest):
        share, rows, columns = (
            density.shape[0] // mesh.shape["ao"],
            density.shape[1] // mesh.shape["gx"],
            density.shape[2] // mesh.shape["ao"],
        )
        fits = columns % LANES == 0 and share % 32 == 0 and rows == 2 * GROUP
        body = jax.shard_map(
            blocked if fits else per_device, mesh=mesh, in_specs=in_specs, out_specs=out_specs, check_vma=False
        )
        return body(density, *rest)

    return run
```

```python
import functools

import jax
import jax.numpy as jnp
from jax import lax
from jax.experimental import pallas as pl
from jax.experimental.pallas import tpu as pltpu
from jax.sharding import PartitionSpec as P

TIME_STEPS = 3


rotation_rate = 0.05


def extended(value, sides, width):
    for axis, dim in sides:
        devices, length = (lax.axis_size(axis), value.shape[dim])
        up = [(i, (i + 1) % devices) for i in range(devices)]
        down = [(j, i) for i, j in up]
        last = lax.slice_in_dim(value, length - width, length, axis=dim)
        leading = lax.slice_in_dim(value, 0, width, axis=dim)
        before = lax.ppermute(last, axis, up)
        after = lax.ppermute(leading, axis, down)
        value = jnp.concatenate([before, value, after], axis=dim)
    return value


def upwind(centre, behind_one, behind_two, ahead_one, ahead_two, direction, speed):
    rear = 0.5 * (3.0 * centre - 4.0 * behind_one + behind_two)
    front = 0.5 * (3.0 * centre - 4.0 * ahead_one + ahead_two)
    return speed * jnp.where(direction == 1, rear, front)


def stencil_matrix(neighbours, weights):
    number = neighbours.shape[0]
    labels = jnp.arange(number, dtype=jnp.int32)
    matches = (neighbours[:, :, None] == labels[None, None, :]).astype(jnp.float32)
    scaled = weights.astype(jnp.float32)
    coupled = jnp.sum(scaled[:, :, None] * matches, axis=1)
    totals = jnp.sum(scaled, axis=1)
    identity = (labels[:, None] == labels[None, :]).astype(jnp.float32)
    return (coupled - totals[:, None] * identity).astype(jnp.bfloat16)


def rotate_block(block, kernel, turn_matrix):
    block_shape = block.shape
    values = block.reshape(block_shape[0], -1)
    potential = jnp.dot(kernel, values, preferred_element_type=jnp.float32)
    wide_values = values.astype(jnp.float32)
    drifted = (wide_values * (1.0 + potential)).astype(jnp.bfloat16)
    turned = jnp.dot(turn_matrix, drifted, preferred_element_type=jnp.float32)
    return (wide_values + rotation_rate * turned).astype(jnp.bfloat16).reshape(block_shape)


def per_device(density, kernel, neighbours, weights, signs, speeds):
    turn_matrix = stencil_matrix(neighbours, weights)
    share = density.shape[0]
    offset = lax.axis_index("ao") * share
    local_signs = lax.dynamic_slice_in_dim(signs, offset, share, 1)
    local_speeds = lax.dynamic_slice_in_dim(speeds, offset, share, 1)
    current = density
    for section_index in range(TIME_STEPS):
        widened = extended(current, (("gx", 1),), 2).astype(jnp.float32)
        centre = current.astype(jnp.float32)
        along_rows = upwind(
            centre,
            widened[:, 1:-3],
            widened[:, :-4],
            widened[:, 3:-1],
            widened[:, 4:],
            local_signs[0][:, None, None],
            local_speeds[0][:, None, None],
        )
        along_columns = upwind(
            centre,
            jnp.roll(centre, 1, 2),
            jnp.roll(centre, 2, 2),
            jnp.roll(centre, -1, 2),
            jnp.roll(centre, -2, 2),
            local_signs[1][:, None, None],
            local_speeds[1][:, None, None],
        )
        advected = (centre - along_rows - along_columns).astype(jnp.bfloat16)
        current = lax.all_to_all(
            rotate_block(
                lax.all_to_all(advected, "ao", split_axis=2, concat_axis=0, tiled=True),
                kernel,
                turn_matrix,
            ),
            "ao",
            split_axis=0,
            concat_axis=2,
            tiled=True,
        )
    return current


LANES = 128
REACH = 2 * TIME_STEPS
GROUP = 8
SLOT = LANES // GROUP
TOGETHER = 4


def pack_kernel(place, main_ref, *refs):
    *side_refs, out_ref, main, sides = refs
    orients, rows, _ = main_ref.shape
    both = len(side_refs) == 2
    width = SLOT if both else GROUP
    slots = LANES // width
    lane = lax.broadcasted_iota(jnp.int32, (orients, LANES), 1)
    owner = ((lane + SLOT // 2) % LANES) // SLOT if both else lane // GROUP

    def flat(ref):
        return ref[...].astype(jnp.float32).reshape(orients * rows, LANES)

    main[...] = flat(main_ref)
    if both:
        wide_lane = lax.broadcasted_iota(jnp.int32, (orients * rows, LANES), 1)
        sides[...] = jnp.where(wide_lane < LANES // 2, flat(side_refs[0]), flat(side_refs[1]))
    else:
        sides[...] = flat(side_refs[0])
    for group in range(rows // slots):
        packed = jnp.zeros((orients, LANES), jnp.float32)
        for slot in range(slots):
            row = group * slots + slot
            out_ref[1 + row] = main[pl.ds(row, orients, stride=rows), :].astype(jnp.bfloat16)
            edge = pltpu.roll(sides[pl.ds(row, orients, stride=rows), :], width * slot, 1)
            packed = jnp.where(owner == slot, edge, packed)
        out_ref[0 if group == 0 else rows + 1] = packed.astype(jnp.bfloat16)


def pack(density, place, shift, part, devices, parts):
    share, rows, columns = density.shape
    tiles = columns // LANES
    offsets = (0, 1) if part else (0, 1, -1)
    length = rows + (1 if part else 2)

    def tile(offset):
        def index(block, place_ref):
            target = lax.rem(place_ref[0] + shift, devices)
            return block, 0, lax.rem(target * parts + part + offset + tiles, tiles)

        return pl.BlockSpec((share, rows, LANES), index)

    return pl.pallas_call(
        pack_kernel,
        grid_spec=pltpu.PrefetchScalarGridSpec(
            num_scalar_prefetch=1,
            grid=(1,),
            in_specs=[tile(offset) for offset in offsets],
            out_specs=pl.BlockSpec((length, share, LANES), lambda block, place_ref: (0, block, 0)),
            scratch_shapes=[pltpu.VMEM((share * rows, LANES), jnp.float32)] * 2,
        ),
        out_shape=jax.ShapeDtypeStruct((length, share, LANES), jnp.bfloat16),
        name="pack",
    )(place, *[density] * len(offsets))


def unpack_kernel(devices, shifts, part, parts, place, *refs):
    blocks, out_ref, wide, staged, sems = refs[: len(shifts)], *refs[-4:]
    rows, share, _ = blocks[0].shape
    copies = []
    for number, shift in enumerate(shifts):
        wide[...] = blocks[number][...].astype(jnp.float32).reshape(rows * share, LANES)
        for orient in range(share):
            staged[number, orient] = wide[pl.ds(orient, rows, stride=share), :].astype(jnp.bfloat16)
        tile = lax.rem(place[0] + shift, devices) * parts + part
        copies.append(
            pltpu.make_async_copy(
                staged.at[number],
                out_ref.at[:, :, pl.ds(pl.multiple_of(tile * LANES, LANES), LANES)],
                sems.at[number],
            )
        )
        copies[-1].start()
    for copy in copies:
        copy.wait()


def unpack(blocks, shifts, place, part, parts, shape, before):
    devices = len(blocks)
    blocks = [blocks[shift] for shift in shifts]
    rows, share, _ = blocks[0].shape
    earlier = () if before is None else (before,)
    return pl.pallas_call(
        functools.partial(unpack_kernel, devices, shifts, part, parts),
        in_specs=[pl.BlockSpec(memory_space=pltpu.SMEM)]
        + [pl.BlockSpec(memory_space=pltpu.VMEM)] * len(shifts)
        + [pl.BlockSpec(memory_space=pl.ANY)] * len(earlier),
        out_specs=pl.BlockSpec(memory_space=pl.ANY),
        scratch_shapes=[
            pltpu.VMEM((rows * share, LANES), jnp.float32),
            pltpu.VMEM((len(shifts), share, rows, LANES), jnp.bfloat16),
            pltpu.SemaphoreType.DMA((len(shifts),)),
        ],
        out_shape=jax.ShapeDtypeStruct(shape, jnp.bfloat16),
        input_output_aliases={1 + len(shifts): 0} if earlier else {},
        compiler_params=pltpu.CompilerParams(vmem_limit_bytes=16 * 2**20),
        name="unpack",
    )(place, *blocks, *earlier)


def steps_kernel(devices, joined, followed, *refs):
    blocks, refs = refs[:devices], refs[devices:]
    above, below, kernel, turn, coefficients = refs[:5]
    edge_in, refs = (refs[5], refs[6:]) if joined else (None, refs[5:])
    outs, refs = refs[:devices], refs[devices:]
    edge_out, refs = (refs[0], refs[1:]) if followed else (None, refs)
    buffers, waiting = refs[:2], refs[2]
    together = waiting.shape[1] // (LANES + 2 * GROUP)
    share = blocks[0].shape[1]
    number = share * devices
    rows = outs[0].shape[0]
    tiles = number // LANES

    def transposed(value_of):
        return jnp.concatenate([value_of(part).astype(jnp.float32) for part in range(devices)], 0).T

    def piece(ref, index, part):
        return ref[index, part * share : (part + 1) * share]

    def fill(first, last, value_of):
        for row in range(first, last):
            cells = transposed(lambda part: value_of(row, part))
            for tile in range(tiles):
                lanes = slice(tile * LANES, (tile + 1) * LANES)
                buffers[0][row + REACH, tile, 2 * GROUP : 2 * GROUP + LANES] = cells[:, lanes]
                if followed:
                    edge_out[row + REACH, tile] = cells[LANES - GROUP :, lanes]

    def fill_sides(first, last, value_of):
        cells = transposed(value_of)
        for row in range(first, last):
            if joined:
                right = GROUP * (row % rows)
            else:
                right = SLOT * (row % GROUP)
                left = (right - GROUP) % LANES
            for tile in range(tiles):
                lanes = slice(tile * LANES, (tile + 1) * LANES)
                buffers[0][row + REACH, tile, GROUP : 2 * GROUP] = (
                    edge_in[row + REACH, tile] if joined else cells[left : left + GROUP, lanes]
                )
                buffers[0][row + REACH, tile, 2 * GROUP + LANES : 3 * GROUP + LANES] = cells[
                    right : right + GROUP, lanes
                ]

    lead = REACH + 1 if joined else REACH
    fill(-REACH, 0, lambda row, part: piece(above, row + lead, part))
    fill(0, rows, lambda row, part: blocks[part][1 + row])
    fill(rows, rows + REACH, lambda row, part: piece(below, 1 + row - rows, part))
    fill_sides(-REACH, 0, lambda part: piece(above, 0 if joined else REACH, part))
    if joined:
        fill_sides(0, rows, lambda part: blocks[part][0])
    else:
        fill_sides(0, GROUP, lambda part: blocks[part][0])
        fill_sides(GROUP, rows, lambda part: blocks[part][rows + 1])
    fill_sides(rows, rows + REACH, lambda part: piece(below, 0, part))

    def advect(source, index, start, length, target):
        for tile in range(tiles):
            lanes = slice(tile * LANES, (tile + 1) * LANES)
            keep, by_row, by_column, row_sign, column_sign = (coefficients[k : k + 1, lanes] for k in range(5))
            forward_row = jnp.broadcast_to(row_sign, (length, LANES)) > 0
            forward_column = jnp.broadcast_to(column_sign, (length, LANES)) > 0
            for half in range(together):

                def at(row, column):
                    return source[index + half + row, tile, start + column : start + column + length]

                row_one = jnp.where(forward_row, at(-1, 0), at(1, 0))
                row_two = jnp.where(forward_row, at(-2, 0), at(2, 0))
                column_one = jnp.where(forward_column, at(0, -1), at(0, 1))
                column_two = jnp.where(forward_column, at(0, -2), at(0, 2))
                value = (
                    keep * at(0, 0)
                    + by_row * (row_one - 0.25 * row_two)
                    + by_column * (column_one - 0.25 * column_two)
                )
                target[half * length : (half + 1) * length, lanes] = value.astype(jnp.bfloat16)

    def rotate(values):
        potential = jnp.dot(values, kernel[...], preferred_element_type=jnp.float32)
        drifted = (values.astype(jnp.float32) * (1.0 + potential)).astype(jnp.bfloat16)
        turned = jnp.dot(drifted, turn[...], preferred_element_type=jnp.float32)
        return (values.astype(jnp.float32) + rotation_rate * turned).astype(jnp.bfloat16)

    for step in range(TIME_STEPS):
        source, target = buffers[step % 2], buffers[(step + 1) % 2]
        last = step == TIME_STEPS - 1
        start, length = (2 * GROUP, LANES) if last else (GROUP, LANES + 2 * GROUP)
        low = 2 * (step + 1)
        turns = (rows + 2 * REACH - 2 * low) // together

        def finish(slot, index):
            result = rotate(waiting[slot, : together * length]).astype(jnp.float32)
            for half in range(together):
                cells = result[half * length : (half + 1) * length]
                if last:
                    back = cells.T.astype(jnp.bfloat16)
                    for part in range(devices):
                        outs[part][index - REACH + half] = back[part * share : (part + 1) * share]
                else:
                    for tile in range(tiles):
                        target[index + half, tile, start : start + length] = cells[
                            :, tile * LANES : (tile + 1) * LANES
                        ]

        advect(source, low, start, length, waiting.at[0])

        @pl.loop(0, turns)
        def _(turn_index):
            index = low + together * turn_index
            slot = lax.rem(turn_index, 2)
            following = jnp.minimum(index + together, low + together * (turns - 1))
            advect(source, following, start, length, waiting.at[1 - slot])
            finish(slot, index)


def three_steps(blocks, above, below, kernel, turn, coefficients, rows, edge, followed):
    devices = len(blocks)
    share = blocks[0].shape[1]
    number = share * devices
    tiles = number // LANES
    tall = rows + 2 * REACH
    vmem = pl.BlockSpec(memory_space=pltpu.VMEM)
    operands = (*blocks, above, below, kernel, turn, coefficients, *([] if edge is None else [edge]))
    out_shape = [jax.ShapeDtypeStruct((rows, share, LANES), jnp.bfloat16)] * devices
    if followed:
        out_shape.append(jax.ShapeDtypeStruct((tall, tiles, GROUP, LANES), jnp.float32))
    outs = pl.pallas_call(
        functools.partial(steps_kernel, devices, edge is not None, followed),
        in_specs=[vmem] * len(operands),
        out_specs=[vmem] * len(out_shape),
        out_shape=out_shape,
        scratch_shapes=[
            *[pltpu.VMEM((tall, tiles, LANES + 4 * GROUP, LANES), jnp.float32)] * 2,
            pltpu.VMEM((2, TOGETHER * (LANES + 2 * GROUP), number), jnp.bfloat16),
        ],
        compiler_params=pltpu.CompilerParams(vmem_limit_bytes=48 * 2**20),
        cost_estimate=pl.CostEstimate(
            flops=12 * number * number * tall * LANES, bytes_accessed=8 * 2**20, transcendentals=0
        ),
        name="three_steps",
    )(*operands)
    return outs[:devices], outs[devices] if followed else None


def blocked(density, kernel, neighbours, weights, signs, speeds):
    devices = lax.axis_size("ao")
    share, rows, columns = density.shape
    parts = columns // devices // LANES
    here = lax.axis_index("ao")
    place = here.astype(jnp.int32).reshape(1)

    packed = [[pack(density, place, shift, part, devices, parts) for shift in range(devices)] for part in range(parts)]

    def turned(value, dim):
        pieces = [
            lax.dynamic_slice_in_dim(value, lax.rem(here - shift + devices, devices) * share, share, dim)
            for shift in range(devices)
        ]
        return jnp.concatenate(pieces, dim)

    turn = turned(turned(stencil_matrix(neighbours, weights), 0), 1)
    kernel = turned(turned(kernel, 0), 1)
    signs, speeds = turned(signs, 1), turned(speeds, 1)

    coefficients = jnp.stack(
        [
            1.0 - 1.5 * (speeds[0] + speeds[1]),
            2.0 * speeds[0],
            2.0 * speeds[1],
            (signs[0] == 1).astype(jnp.float32),
            (signs[1] == 1).astype(jnp.float32),
        ]
    )
    kernel, turn = kernel.T, turn.T

    size = lax.axis_size("gx")
    up = [(i, (i + 1) % size) for i in range(size)]
    down = [(j, i) for i, j in up]
    def ahead(value, shift):
        return lax.ppermute(value, "ao", [(i, (i + shift) % devices) for i in range(devices)])

    def after(value, *earlier):
        return lax.optimization_barrier((value, *earlier))[0]

    received = []
    for part in range(parts):
        blocks = packed[part]
        if received:
            earlier = received[-1]
            blocks = [after(block, early) for block, early in zip(blocks, earlier)]
        received.append([blocks[0]] + [ahead(blocks[shift], shift) for shift in range(1, devices)])
    results, edge = [], None
    for part in range(parts):
        arrived = received[part]
        ends = [after(block, results[-1]) for block in arrived] if results else arrived

        def joint(first, last):
            return jnp.concatenate([block[first:last] for block in ends], 1)

        length = ends[0].shape[0]
        if part:
            upper = jnp.concatenate([joint(0, 1), joint(length - REACH, length)], 0)
        else:
            upper = joint(length - REACH - 1, length)
        above = lax.ppermute(upper, "gx", up)
        below = lax.ppermute(joint(0, REACH + 1), "gx", down)
        result, edge = three_steps(
            arrived, above, below, kernel, turn, coefficients, rows, edge, part + 1 < parts
        )
        results.append(result)
    evolved = None
    for part in range(parts):
        result = results[part]
        returned = [result[0]] + [ahead(result[shift], devices - shift) for shift in range(1, devices)]
        middle = devices // 2 if part + 1 == parts else devices
        for shifts in (range(middle), range(middle, devices)):
            if len(shifts):
                evolved = unpack(returned, shifts, place, part, parts, density.shape, evolved)
    return evolved


def solution(mesh):
    in_specs = (P("ao", "gx", None), P(), P(), P(), P(), P())
    out_specs = P("ao", "gx", None)

    def run(density, *rest):
        share, rows, columns = (
            density.shape[0] // mesh.shape["ao"],
            density.shape[1] // mesh.shape["gx"],
            density.shape[2] // mesh.shape["ao"],
        )
        fits = columns % LANES == 0 and share % 32 == 0 and rows == 2 * GROUP
        body = jax.shard_map(
            blocked if fits else per_device, mesh=mesh, in_specs=in_specs, out_specs=out_specs, check_vma=False
        )
        return body(density, *rest)

    return run
```

```python
import functools

import jax
import jax.numpy as jnp
from jax import lax
from jax.experimental import pallas as pl
from jax.experimental.pallas import tpu as pltpu
from jax.sharding import PartitionSpec as P

TIME_STEPS = 3


rotation_rate = 0.05


def extended(value, sides, width):
    for axis, dim in sides:
        devices, length = (lax.axis_size(axis), value.shape[dim])
        up = [(i, (i + 1) % devices) for i in range(devices)]
        down = [(j, i) for i, j in up]
        last = lax.slice_in_dim(value, length - width, length, axis=dim)
        leading = lax.slice_in_dim(value, 0, width, axis=dim)
        before = lax.ppermute(last, axis, up)
        after = lax.ppermute(leading, axis, down)
        value = jnp.concatenate([before, value, after], axis=dim)
    return value


def upwind(centre, behind_one, behind_two, ahead_one, ahead_two, direction, speed):
    rear = 0.5 * (3.0 * centre - 4.0 * behind_one + behind_two)
    front = 0.5 * (3.0 * centre - 4.0 * ahead_one + ahead_two)
    return speed * jnp.where(direction == 1, rear, front)


def stencil_matrix(neighbours, weights):
    number = neighbours.shape[0]
    labels = jnp.arange(number, dtype=jnp.int32)
    matches = (neighbours[:, :, None] == labels[None, None, :]).astype(jnp.float32)
    scaled = weights.astype(jnp.float32)
    coupled = jnp.sum(scaled[:, :, None] * matches, axis=1)
    totals = jnp.sum(scaled, axis=1)
    identity = (labels[:, None] == labels[None, :]).astype(jnp.float32)
    return (coupled - totals[:, None] * identity).astype(jnp.bfloat16)


def rotate_block(block, kernel, turn_matrix):
    block_shape = block.shape
    values = block.reshape(block_shape[0], -1)
    potential = jnp.dot(kernel, values, preferred_element_type=jnp.float32)
    wide_values = values.astype(jnp.float32)
    drifted = (wide_values * (1.0 + potential)).astype(jnp.bfloat16)
    turned = jnp.dot(turn_matrix, drifted, preferred_element_type=jnp.float32)
    return (wide_values + rotation_rate * turned).astype(jnp.bfloat16).reshape(block_shape)


def per_device(density, kernel, neighbours, weights, signs, speeds):
    turn_matrix = stencil_matrix(neighbours, weights)
    share = density.shape[0]
    offset = lax.axis_index("ao") * share
    local_signs = lax.dynamic_slice_in_dim(signs, offset, share, 1)
    local_speeds = lax.dynamic_slice_in_dim(speeds, offset, share, 1)
    current = density
    for section_index in range(TIME_STEPS):
        widened = extended(current, (("gx", 1),), 2).astype(jnp.float32)
        centre = current.astype(jnp.float32)
        along_rows = upwind(
            centre,
            widened[:, 1:-3],
            widened[:, :-4],
            widened[:, 3:-1],
            widened[:, 4:],
            local_signs[0][:, None, None],
            local_speeds[0][:, None, None],
        )
        along_columns = upwind(
            centre,
            jnp.roll(centre, 1, 2),
            jnp.roll(centre, 2, 2),
            jnp.roll(centre, -1, 2),
            jnp.roll(centre, -2, 2),
            local_signs[1][:, None, None],
            local_speeds[1][:, None, None],
        )
        advected = (centre - along_rows - along_columns).astype(jnp.bfloat16)
        current = lax.all_to_all(
            rotate_block(
                lax.all_to_all(advected, "ao", split_axis=2, concat_axis=0, tiled=True),
                kernel,
                turn_matrix,
            ),
            "ao",
            split_axis=0,
            concat_axis=2,
            tiled=True,
        )
    return current


LANES = 128
REACH = 2 * TIME_STEPS
GROUP = 8
SLOT = LANES // GROUP
TOGETHER = 4


def pack_kernel(place, main_ref, *refs):
    *side_refs, out_ref, main, sides = refs
    orients, rows, _ = main_ref.shape
    both = len(side_refs) == 2
    width = SLOT if both else GROUP
    slots = LANES // width
    lane = lax.broadcasted_iota(jnp.int32, (orients, LANES), 1)
    owner = ((lane + SLOT // 2) % LANES) // SLOT if both else lane // GROUP

    def flat(ref):
        return ref[...].astype(jnp.float32).reshape(orients * rows, LANES)

    main[...] = flat(main_ref)
    if both:
        wide_lane = lax.broadcasted_iota(jnp.int32, (orients * rows, LANES), 1)
        sides[...] = jnp.where(wide_lane < LANES // 2, flat(side_refs[0]), flat(side_refs[1]))
    else:
        sides[...] = flat(side_refs[0])
    for group in range(rows // slots):
        packed = jnp.zeros((orients, LANES), jnp.float32)
        for slot in range(slots):
            row = group * slots + slot
            out_ref[1 + row] = main[pl.ds(row, orients, stride=rows), :].astype(jnp.bfloat16)
            edge = pltpu.roll(sides[pl.ds(row, orients, stride=rows), :], width * slot, 1)
            packed = jnp.where(owner == slot, edge, packed)
        out_ref[0 if group == 0 else rows + 1] = packed.astype(jnp.bfloat16)


def pack(density, place, shift, part, devices, parts):
    share, rows, columns = density.shape
    tiles = columns // LANES
    offsets = (0, 1) if part else (0, 1, -1)
    length = rows + (1 if part else 2)

    def tile(offset):
        def index(block, place_ref):
            target = lax.rem(place_ref[0] + shift, devices)
            return block, 0, lax.rem(target * parts + part + offset + tiles, tiles)

        return pl.BlockSpec((share, rows, LANES), index)

    return pl.pallas_call(
        pack_kernel,
        grid_spec=pltpu.PrefetchScalarGridSpec(
            num_scalar_prefetch=1,
            grid=(1,),
            in_specs=[tile(offset) for offset in offsets],
            out_specs=pl.BlockSpec((length, share, LANES), lambda block, place_ref: (0, block, 0)),
            scratch_shapes=[pltpu.VMEM((share * rows, LANES), jnp.float32)] * 2,
        ),
        out_shape=jax.ShapeDtypeStruct((length, share, LANES), jnp.bfloat16),
        name="pack",
    )(place, *[density] * len(offsets))


def unpack_kernel(devices, shifts, part, parts, place, *refs):
    blocks, out_ref, wide, staged, sems = refs[: len(shifts)], *refs[-4:]
    rows, share, _ = blocks[0].shape
    copies = []
    for number, shift in enumerate(shifts):
        wide[...] = blocks[number][...].astype(jnp.float32).reshape(rows * share, LANES)
        for orient in range(share):
            staged[number, orient] = wide[pl.ds(orient, rows, stride=share), :].astype(jnp.bfloat16)
        tile = lax.rem(place[0] + shift, devices) * parts + part
        copies.append(
            pltpu.make_async_copy(
                staged.at[number],
                out_ref.at[:, :, pl.ds(pl.multiple_of(tile * LANES, LANES), LANES)],
                sems.at[number],
            )
        )
        copies[-1].start()
    for copy in copies:
        copy.wait()


def unpack(blocks, shifts, place, part, parts, shape, before):
    devices = len(blocks)
    blocks = [blocks[shift] for shift in shifts]
    rows, share, _ = blocks[0].shape
    earlier = () if before is None else (before,)
    return pl.pallas_call(
        functools.partial(unpack_kernel, devices, shifts, part, parts),
        in_specs=[pl.BlockSpec(memory_space=pltpu.SMEM)]
        + [pl.BlockSpec(memory_space=pltpu.VMEM)] * len(shifts)
        + [pl.BlockSpec(memory_space=pl.ANY)] * len(earlier),
        out_specs=pl.BlockSpec(memory_space=pl.ANY),
        scratch_shapes=[
            pltpu.VMEM((rows * share, LANES), jnp.float32),
            pltpu.VMEM((len(shifts), share, rows, LANES), jnp.bfloat16),
            pltpu.SemaphoreType.DMA((len(shifts),)),
        ],
        out_shape=jax.ShapeDtypeStruct(shape, jnp.bfloat16),
        input_output_aliases={1 + len(shifts): 0} if earlier else {},
        compiler_params=pltpu.CompilerParams(vmem_limit_bytes=16 * 2**20),
        name="unpack",
    )(place, *blocks, *earlier)


def steps_kernel(devices, joined, followed, *refs):
    blocks, refs = refs[:devices], refs[devices:]
    above, below, kernel, turn, coefficients = refs[:5]
    edge_in, refs = (refs[5], refs[6:]) if joined else (None, refs[5:])
    outs, refs = refs[:devices], refs[devices:]
    edge_out, refs = (refs[0], refs[1:]) if followed else (None, refs)
    buffers, waiting = refs[:2], refs[2]
    together = waiting.shape[1] // (LANES + 2 * GROUP)
    share = blocks[0].shape[1]
    number = share * devices
    rows = outs[0].shape[0]
    tiles = number // LANES

    def transposed(value_of):
        return jnp.concatenate([value_of(part).astype(jnp.float32) for part in range(devices)], 0).T

    def piece(ref, index, part):
        return ref[index, part * share : (part + 1) * share]

    def fill(first, last, value_of):
        for row in range(first, last):
            cells = transposed(lambda part: value_of(row, part))
            for tile in range(tiles):
                lanes = slice(tile * LANES, (tile + 1) * LANES)
                buffers[0][row + REACH, tile, 2 * GROUP : 2 * GROUP + LANES] = cells[:, lanes]
                if followed:
                    edge_out[row + REACH, tile] = cells[LANES - GROUP :, lanes]

    def fill_sides(first, last, value_of):
        cells = transposed(value_of)
        for row in range(first, last):
            if joined:
                right = GROUP * (row % rows)
            else:
                right = SLOT * (row % GROUP)
                left = (right - GROUP) % LANES
            for tile in range(tiles):
                lanes = slice(tile * LANES, (tile + 1) * LANES)
                buffers[0][row + REACH, tile, GROUP : 2 * GROUP] = (
                    edge_in[row + REACH, tile] if joined else cells[left : left + GROUP, lanes]
                )
                buffers[0][row + REACH, tile, 2 * GROUP + LANES : 3 * GROUP + LANES] = cells[
                    right : right + GROUP, lanes
                ]

    lead = REACH + 1 if joined else REACH
    fill(-REACH, 0, lambda row, part: piece(above, row + lead, part))
    fill(0, rows, lambda row, part: blocks[part][1 + row])
    fill(rows, rows + REACH, lambda row, part: piece(below, 1 + row - rows, part))
    fill_sides(-REACH, 0, lambda part: piece(above, 0 if joined else REACH, part))
    if joined:
        fill_sides(0, rows, lambda part: blocks[part][0])
    else:
        fill_sides(0, GROUP, lambda part: blocks[part][0])
        fill_sides(GROUP, rows, lambda part: blocks[part][rows + 1])
    fill_sides(rows, rows + REACH, lambda part: piece(below, 0, part))

    def advect(source, index, start, length, target):
        for tile in range(tiles):
            lanes = slice(tile * LANES, (tile + 1) * LANES)
            keep, by_row, by_column, row_sign, column_sign = (coefficients[k : k + 1, lanes] for k in range(5))
            forward_row = jnp.broadcast_to(row_sign, (length, LANES)) > 0
            forward_column = jnp.broadcast_to(column_sign, (length, LANES)) > 0
            for half in range(together):

                def at(row, column):
                    return source[index + half + row, tile, start + column : start + column + length]

                row_one = jnp.where(forward_row, at(-1, 0), at(1, 0))
                row_two = jnp.where(forward_row, at(-2, 0), at(2, 0))
                column_one = jnp.where(forward_column, at(0, -1), at(0, 1))
                column_two = jnp.where(forward_column, at(0, -2), at(0, 2))
                value = (
                    keep * at(0, 0)
                    + by_row * (row_one - 0.25 * row_two)
                    + by_column * (column_one - 0.25 * column_two)
                )
                target[half * length : (half + 1) * length, lanes] = value.astype(jnp.bfloat16)

    def rotate(values):
        potential = jnp.dot(values, kernel[...], preferred_element_type=jnp.float32)
        drifted = (values.astype(jnp.float32) * (1.0 + potential)).astype(jnp.bfloat16)
        turned = jnp.dot(drifted, turn[...], preferred_element_type=jnp.float32)
        return (values.astype(jnp.float32) + rotation_rate * turned).astype(jnp.bfloat16)

    for step in range(TIME_STEPS):
        source, target = buffers[step % 2], buffers[(step + 1) % 2]
        last = step == TIME_STEPS - 1
        start, length = (2 * GROUP, LANES) if last else (GROUP, LANES + 2 * GROUP)
        low = 2 * (step + 1)
        turns = (rows + 2 * REACH - 2 * low) // together

        def finish(slot, index):
            result = rotate(waiting[slot, : together * length]).astype(jnp.float32)
            for half in range(together):
                cells = result[half * length : (half + 1) * length]
                if last:
                    back = cells.T.astype(jnp.bfloat16)
                    for part in range(devices):
                        outs[part][index - REACH + half] = back[part * share : (part + 1) * share]
                else:
                    for tile in range(tiles):
                        target[index + half, tile, start : start + length] = cells[
                            :, tile * LANES : (tile + 1) * LANES
                        ]

        advect(source, low, start, length, waiting.at[0])

        @pl.loop(0, turns)
        def _(turn_index):
            index = low + together * turn_index
            slot = lax.rem(turn_index, 2)
            following = jnp.minimum(index + together, low + together * (turns - 1))
            advect(source, following, start, length, waiting.at[1 - slot])
            finish(slot, index)


def three_steps(blocks, above, below, kernel, turn, coefficients, rows, edge, followed):
    devices = len(blocks)
    share = blocks[0].shape[1]
    number = share * devices
    tiles = number // LANES
    tall = rows + 2 * REACH
    vmem = pl.BlockSpec(memory_space=pltpu.VMEM)
    operands = (*blocks, above, below, kernel, turn, coefficients, *([] if edge is None else [edge]))
    out_shape = [jax.ShapeDtypeStruct((rows, share, LANES), jnp.bfloat16)] * devices
    if followed:
        out_shape.append(jax.ShapeDtypeStruct((tall, tiles, GROUP, LANES), jnp.float32))
    outs = pl.pallas_call(
        functools.partial(steps_kernel, devices, edge is not None, followed),
        in_specs=[vmem] * len(operands),
        out_specs=[vmem] * len(out_shape),
        out_shape=out_shape,
        scratch_shapes=[
            *[pltpu.VMEM((tall, tiles, LANES + 4 * GROUP, LANES), jnp.float32)] * 2,
            pltpu.VMEM((2, TOGETHER * (LANES + 2 * GROUP), number), jnp.bfloat16),
        ],
        compiler_params=pltpu.CompilerParams(vmem_limit_bytes=48 * 2**20),
        cost_estimate=pl.CostEstimate(
            flops=12 * number * number * tall * LANES, bytes_accessed=8 * 2**20, transcendentals=0
        ),
        name="three_steps",
    )(*operands)
    return outs[:devices], outs[devices] if followed else None


def blocked(density, kernel, neighbours, weights, signs, speeds):
    devices = lax.axis_size("ao")
    share, rows, columns = density.shape
    parts = columns // devices // LANES
    here = lax.axis_index("ao")
    place = here.astype(jnp.int32).reshape(1)

    packed = [[pack(density, place, shift, part, devices, parts) for shift in range(devices)] for part in range(parts)]

    def turned(value, dim):
        pieces = [
            lax.dynamic_slice_in_dim(value, lax.rem(here - shift + devices, devices) * share, share, dim)
            for shift in range(devices)
        ]
        return jnp.concatenate(pieces, dim)

    turn = turned(turned(stencil_matrix(neighbours, weights), 0), 1)
    kernel = turned(turned(kernel, 0), 1)
    signs, speeds = turned(signs, 1), turned(speeds, 1)

    coefficients = jnp.stack(
        [
            1.0 - 1.5 * (speeds[0] + speeds[1]),
            2.0 * speeds[0],
            2.0 * speeds[1],
            (signs[0] == 1).astype(jnp.float32),
            (signs[1] == 1).astype(jnp.float32),
        ]
    )
    kernel, turn = kernel.T, turn.T

    size = lax.axis_size("gx")
    up = [(i, (i + 1) % size) for i in range(size)]
    down = [(j, i) for i, j in up]
    def ahead(value, shift):
        return lax.ppermute(value, "ao", [(i, (i + shift) % devices) for i in range(devices)])

    def after(value, *earlier):
        return lax.optimization_barrier((value, *earlier))[0]

    received = []
    for part in range(parts):
        blocks = packed[part]
        if received:
            earlier = received[-1]
            blocks = [after(block, early) for block, early in zip(blocks, earlier)]
        received.append([blocks[0]] + [ahead(blocks[shift], shift) for shift in range(1, devices)])
    results, edge = [], None
    for part in range(parts):
        arrived = received[part]
        ends = [after(block, results[-1]) for block in arrived] if results else arrived

        def joint(first, last):
            return jnp.concatenate([block[first:last] for block in ends], 1)

        length = ends[0].shape[0]
        if part:
            upper = jnp.concatenate([joint(0, 1), joint(length - REACH, length)], 0)
        else:
            upper = joint(length - REACH - 1, length)
        above = lax.ppermute(upper, "gx", up)
        below = lax.ppermute(joint(0, REACH + 1), "gx", down)
        result, edge = three_steps(
            arrived, above, below, kernel, turn, coefficients, rows, edge, part + 1 < parts
        )
        results.append(result)
    evolved = None
    for part in range(parts):
        result = results[part]
        returned = [result[0]] + [ahead(result[shift], devices - shift) for shift in range(1, devices)]
        middle = devices // 2 if part + 1 == parts else devices
        for shifts in (range(middle), *[(shift,) for shift in range(middle, devices)]):
            if len(shifts):
                evolved = unpack(returned, shifts, place, part, parts, density.shape, evolved)
    return evolved


def solution(mesh):
    in_specs = (P("ao", "gx", None), P(), P(), P(), P(), P())
    out_specs = P("ao", "gx", None)

    def run(density, *rest):
        share, rows, columns = (
            density.shape[0] // mesh.shape["ao"],
            density.shape[1] // mesh.shape["gx"],
            density.shape[2] // mesh.shape["ao"],
        )
        fits = columns % LANES == 0 and share % 32 == 0 and rows == 2 * GROUP
        body = jax.shard_map(
            blocked if fits else per_device, mesh=mesh, in_specs=in_specs, out_specs=out_specs, check_vma=False
        )
        return body(density, *rest)

    return run
```
